1024 devices in a mesh: blk: 256 (over z_lo, x, y), grp: 4 (over z_hi, core).
Axes of the slice: x: 4, y: 4, z: 32 (z_hi: 2, z_lo: 16; z = z_hi * 16 + z_lo), core: 2. Of those that a mesh axis runs over, the one named last changes fastest.
Arguments:
- image_emb: float32 [131072, 1152], P(('blk', 'grp')), may hold values from -0.1875 to 0.1875
- text_emb: float32 [131072, 1152], P(('blk', 'grp')), may hold values from -0.1875 to 0.1875
- log_scale: float32 [1], replicated, may hold values from 1.5 to 2.5
- bias: float32 [1], replicated, may hold values from -3 to 0
Outputs:
- row_loss: float32 [131072], P(('blk', 'grp'))
- image_grad: float32 [131072, 1152], P(('blk', 'grp'))
- text_grad: float32 [131072, 1152], P(('blk', 'grp'))
The draws below stay inside these ranges and needn't reach their ends.
All inputs are finite; a program needn't handle non-finite values.
Results may differ from the reference program's by a relative error of at most 0.012.
Values may be sent and summed in bfloat16 or wider, within the bound.
A program may use at most 32 MiB of HBM per device.

```python
import jax
import jax.numpy as jnp
from jax import lax

D = 1152
ROWS = 128
SPAN = 4
BATCH = 131072
N_BLK = 256
N_GRP = 4


def shard_levels(own_key, shape, cuts, low, top_value):
    factor_of = 1.0
    for axis_at, parts in cuts:
        steps = jax.random.uniform(jax.random.fold_in(jax.random.fold_in(own_key, 6), axis_at), (parts,), jnp.float32, low / len(cuts), top_value / len(cuts))
        factor_of = factor_of * jnp.repeat(jnp.exp(steps), shape[axis_at] // parts).reshape((-1,) + (1,) * (len(shape) - 1 - axis_at))
    return factor_of


def gaussian(own_key, dims, width, reach, shards=(), kind=jnp.bfloat16):
    level = shard_levels(own_key, dims, shards, -0.22, 0.18) if shards else 1.0
    array = jax.random.normal(own_key, dims, jnp.float32) * width * level
    return jnp.minimum(jnp.maximum(array, -reach), reach).astype(kind)


def setup_inputs(seed: int = 0) -> dict:
    arg_keys = jax.random.split(jax.random.key(seed), 5)
    image_emb = gaussian(arg_keys[0], (BATCH, D), 0.03, 0.1875, ((0, 1024),), jnp.float32)
    text_emb = gaussian(arg_keys[1], (BATCH, D), 0.03, 0.1875, ((0, 1024),), jnp.float32)
    log_scale = jnp.clip(jax.random.uniform(arg_keys[2], (1,), jnp.float32, 1.5, 2.5), 1.5, 2.5)
    bias = jnp.clip(jax.random.uniform(arg_keys[3], (1,), jnp.float32, -3.0, 0.0), -3.0, 0.0)
    return {"image_emb": image_emb, "text_emb": text_emb, "log_scale": log_scale, "bias": bias}


def unit_rows(emb):
    norms = jnp.sqrt(lax.optimization_barrier(jnp.sum(emb * emb, axis=1, keepdims=True)) + 1e-06)
    return (emb / norms, norms)

def unit_backward(unit, norms, grad):
    return (grad - unit * lax.optimization_barrier(jnp.sum(unit * grad, axis=1, keepdims=True))) / norms

def reference(image_emb, text_emb, log_scale, bias):
    nblocks = N_BLK * N_GRP
    scale = jnp.exp(log_scale[0])
    offset = bias[0]
    image_unit, image_norm = unit_rows(image_emb)
    text_unit, text_norm = unit_rows(text_emb)
    image_half = image_unit.astype(jnp.bfloat16)
    text_half = text_unit.astype(jnp.bfloat16)
    image_blocks = image_half.reshape(nblocks, ROWS, D).astype(jnp.float32)
    diagonal = 2.0 * jnp.eye(ROWS, dtype=jnp.float32) - 1.0
    loss_total = jnp.zeros((nblocks, ROWS), jnp.float32)
    image_acc = jnp.zeros((nblocks, ROWS, D), jnp.float32)
    text_acc = jnp.zeros((nblocks * ROWS, D), jnp.float32)
    for shift_by in range(-SPAN, SPAN + 1):
        text_blocks = jnp.roll(text_half, -shift_by * ROWS, axis=0).reshape(nblocks, ROWS, D).astype(jnp.float32)
        logits = scale * jnp.einsum('nrd,nsd->nrs', image_blocks, text_blocks) + offset
        signs = diagonal if shift_by == 0 else jnp.float32(-1.0)
        loss_total = loss_total + lax.optimization_barrier(jnp.sum(jax.nn.softplus(-signs * logits), axis=2))
        coeff = (-scale * signs * jax.nn.sigmoid(-signs * logits)).astype(jnp.bfloat16)
        coeff = lax.optimization_barrier(coeff).astype(jnp.float32)
        image_acc = image_acc + jnp.einsum('nrs,nsd->nrd', coeff, text_blocks)
        partial_text = jnp.einsum('nrs,nrd->nsd', coeff, image_blocks).reshape(nblocks * ROWS, D)
        text_acc = text_acc + jnp.roll(partial_text, shift_by * ROWS, axis=0)
    row_loss = loss_total.reshape(nblocks * ROWS) / ((2 * SPAN + 1) * ROWS)
    image_grad = unit_backward(image_unit, image_norm, image_acc.reshape(nblocks * ROWS, D))
    text_grad = unit_backward(text_unit, text_norm, text_acc)
    return (row_loss, image_grad, text_grad)
```

```python
import jax
import jax.numpy as jnp
from jax import lax
from jax.experimental import pallas as pl
from jax.experimental.pallas import tpu as pltpu
from jax.sharding import PartitionSpec as P

MESH = pl.DeviceIdType.MESH
F32 = jnp.float32
BF16 = jnp.bfloat16

ROWS = 128
WIDTH = 1152
BLOCKS = 9
NZ = 32
CHUNKS = 4
CH = ROWS // CHUNKS

OWN, SIB, PREV, NEXT, EDGE = range(5)


def kernel(
    img_ref, txt_ref, ls_ref, bias_ref,
    loss_ref, gimg_ref, gtxt_ref,
    early, ring, late_r, late_y, acc, loss_acc,
    ring_s, ring_r, next_s, next_r, prev_s, prev_r, sib_s, sib_r,
    fy_s, fy_r, rs_s, rs_r, ys_s, ys_r,
):
    blk, grp = lax.axis_index("blk"), lax.axis_index("grp")
    zhi, core = grp // 2, grp % 2
    zlo, xy = blk // 16, blk % 16
    z = zhi * 16 + zlo

    def at_z(zz):
        return {"blk": (zz % 16) * 16 + xy, "grp": (zz // 16) * 2 + core}

    up, down = at_z((z + 1) % NZ), at_z((z + NZ - 1) % NZ)
    side = 1 - 2 * zhi
    after = {"blk": (blk + side + 256) % 256, "grp": grp}
    before = {"blk": (blk - side + 256) % 256, "grp": grp}
    sibling = {"blk": blk, "grp": grp + 1 - 2 * core}
    role = core + zhi - 2 * core * zhi

    barrier = pltpu.get_barrier_semaphore()
    for dev in (up, down, after, before, sibling):
        pl.semaphore_signal(barrier, inc=1, device_id=dev, device_id_type=MESH)

    for src, i in ((img_ref, 0), (txt_ref, 1)):
        for c in range(CHUNKS):
            r = pl.ds(c * CH, CH)
            x = src[r, :]
            inv = lax.rsqrt(jnp.sum(x * x, axis=1, keepdims=True) + 1e-06)
            early[OWN, i, r, :] = (x * inv).astype(BF16)
    acc[...] = jnp.zeros_like(acc)
    loss_acc[...] = jnp.zeros_like(loss_acc)
    scale = jnp.exp(jnp.full((1, 128), ls_ref[0], F32))
    offset = bias_ref[0]

    pl.semaphore_wait(barrier, 5)

    def remote(src, dst, ss, rs, dev):
        return pltpu.make_async_remote_copy(
            src_ref=src, dst_ref=dst, send_sem=ss, recv_sem=rs, device_id=dev, device_id_type=MESH
        )

    def rows(j):
        return pl.ds(j * CH, CH)

    def hop(h, d, j, first=False, last=False):
        if first:
            src = early.at[OWN if j < CHUNKS // 2 else NEXT, d, rows(j)]
        else:
            src = ring.at[h - 1, d, rows(j)]
        dst = late_r.at[d, rows(j)] if last else ring.at[h, d, rows(j)]
        return remote(src, dst, ring_s.at[h, d, j], ring_r.at[h, d, j], up if d == 0 else down)

    def to_before(d, j):
        return remote(
            early.at[OWN, d, rows(j)], early.at[NEXT, d, rows(j)], next_s.at[d, j], next_r.at[d, j], before
        )

    def to_after(d):
        return remote(early.at[OWN, d], early.at[PREV, d], prev_s.at[d], prev_r.at[d], after)

    own_to_sib = remote(early.at[OWN], early.at[SIB], sib_s.at[0], sib_r.at[0], sibling)
    edge_to_sib = remote(early.at[NEXT - role], early.at[EDGE], sib_s.at[1], sib_r.at[1], sibling)

    for j in range(CHUNKS // 2):
        for d in range(2):
            hop(0, d, j, first=True).start()
            to_before(d, j + CHUNKS // 2).start()
    own_to_sib.start()
    for d in range(2):
        to_after(d).start()
        for j in range(CHUNKS // 2):
            to_before(d, j).start()
    for j in range(CHUNKS // 2, CHUNKS):
        for d in range(2):
            to_before(d, j).wait_recv()
            hop(0, d, j, first=True).start()

    def forward(h, last=False):
        for j in range(CHUNKS):
            for d in range(2):
                hop(h - 1, d, j, first=True).wait_recv()
                hop(h, d, j, last=last).start()

    def unit(i, y, diagonal=None):
        s = lax.dot_general(
            early[OWN, i], y, (((1,), (1,)), ((), ())), preferred_element_type=F32
        )
        u = scale * s + offset
        if diagonal is not None:
            same = lax.broadcasted_iota(jnp.int32, u.shape, 0) == lax.broadcasted_iota(jnp.int32, u.shape, 1)
            flip = jnp.where(same, 1.0 - 2.0 * diagonal, 1.0)
            u = u * flip
        e = jnp.exp(-jnp.abs(u))
        c = scale * (jnp.where(u >= 0, 1.0, e) / (1.0 + e))
        if diagonal is not None:
            c = c * flip
        acc[i] += jnp.dot(c.astype(BF16), y, preferred_element_type=F32)
        if i == 0:
            loss_acc[...] += jnp.maximum(u, 0.0) + jnp.log1p(e)

    def plain(h, _):
        forward(h)
        return _

    lax.fori_loop(1, 6, plain, 0)

    own_to_sib.wait_recv()
    for d in range(2):
        to_after(d).wait_recv()
        for j in range(CHUNKS // 2):
            to_before(d, j).wait_recv()
    edge_to_sib.start()

    def with_unit(p, _):
        diagonal = jnp.where(p == 0, 1.0, 0.0).astype(F32)
        forward(6 + 2 * p)
        unit(0, early[p, 1], diagonal)
        forward(7 + 2 * p)
        unit(1, early[p, 0], diagonal)
        return _

    lax.fori_loop(0, 4, with_unit, 0)
    edge_to_sib.wait_recv()
    forward(14)
    unit(0, early[EDGE, 1])
    forward(15, last=True)
    unit(1, early[EDGE, 0])

    def fwd_y(d, j):
        return remote(
            late_r.at[d, rows(j)], late_y.at[d, rows(j)], fy_s.at[d, j], fy_r.at[d, j],
            after if j < CHUNKS // 2 else before,
        )

    def fwd_rs(d, j):
        return remote(
            late_r.at[d, rows(j)], late_r.at[d, rows(CHUNKS + j)], rs_s.at[d, j], rs_r.at[d, j], sibling
        )

    def fwd_ys(d, j):
        return remote(
            late_y.at[d, rows(j)], late_y.at[d, rows(CHUNKS + j)], ys_s.at[d, j], ys_r.at[d, j], sibling
        )

    chunks = [(d, j) for j in range(CHUNKS) for d in range(2)]
    for d, j in chunks:
        hop(15, d, j, first=True, last=True).wait_recv()
        fwd_y(d, j).start()
        fwd_rs(d, j).start()
    lo, hi = pl.ds(0, ROWS), pl.ds(ROWS, ROWS)
    for i in range(2):
        unit(i, late_r[1 - i, lo])
    for d, j in chunks:
        fwd_y(d, j).wait_recv()
        fwd_ys(d, j).start()
    for d, j in chunks:
        fwd_rs(d, j).wait_recv()
    for i in range(2):
        unit(i, late_r[1 - i, hi])
        unit(i, late_y[1 - i, lo])
    for d, j in chunks:
        fwd_ys(d, j).wait_recv()
    for i in range(2):
        unit(i, late_y[1 - i, hi])

    for src, dst, i in ((img_ref, gimg_ref, 0), (txt_ref, gtxt_ref, 1)):
        for c in range(CHUNKS):
            r = pl.ds(c * CH, CH)
            x = src[r, :]
            g = acc[i, r, :]
            inv = lax.rsqrt(jnp.sum(x * x, axis=1, keepdims=True) + 1e-06)
            x = x * inv
            dst[r, :] = (g - x * jnp.sum(x * g, axis=1, keepdims=True)) * inv
    loss_ref[...] = jnp.sum(loss_acc[...].T, axis=0) / (BLOCKS * ROWS)

    def sent(h, _):
        for d in range(2):
            for j in range(CHUNKS):
                hop(h, d, j, first=True).wait_send()
        return _

    lax.fori_loop(0, 15, sent, 0)
    for d, j in chunks:
        hop(15, d, j, first=True, last=True).wait_send()
        to_before(d, j).wait_send()
        fwd_y(d, j).wait_send()
        fwd_rs(d, j).wait_send()
        fwd_ys(d, j).wait_send()
    for d in range(2):
        to_after(d).wait_send()
    own_to_sib.wait_send()
    edge_to_sib.wait_send()


def on_device(image_emb, text_emb, log_scale, bias):
    vmem, smem = pl.BlockSpec(memory_space=pltpu.VMEM), pl.BlockSpec(memory_space=pltpu.SMEM)
    dma = pltpu.SemaphoreType.DMA
    return pl.pallas_call(
        kernel,
        out_shape=(
            jax.ShapeDtypeStruct((ROWS,), F32),
            jax.ShapeDtypeStruct((ROWS, WIDTH), F32),
            jax.ShapeDtypeStruct((ROWS, WIDTH), F32),
        ),
        in_specs=[vmem, vmem, smem, smem],
        out_specs=(vmem, vmem, vmem),
        scratch_shapes=[
            pltpu.VMEM((5, 2, ROWS, WIDTH), BF16),
            pltpu.VMEM((15, 2, ROWS, WIDTH), BF16),
            pltpu.VMEM((2, 2 * ROWS, WIDTH), BF16),
            pltpu.VMEM((2, 2 * ROWS, WIDTH), BF16),
            pltpu.VMEM((2, ROWS, WIDTH), F32),
            pltpu.VMEM((ROWS, ROWS), F32),
            dma((16, 2, CHUNKS)), dma((16, 2, CHUNKS)),
            dma((2, CHUNKS)), dma((2, CHUNKS)),
            dma((2,)), dma((2,)),
            dma((2,)), dma((2,)),
            dma((2, CHUNKS)), dma((2, CHUNKS)),
            dma((2, CHUNKS)), dma((2, CHUNKS)),
            dma((2, CHUNKS)), dma((2, CHUNKS)),
        ],
        compiler_params=pltpu.CompilerParams(
            collective_id=0, has_side_effects=True, vmem_limit_bytes=40 * 2**20
        ),
    )(image_emb, text_emb, log_scale, bias)


def solution(mesh):
    in_specs = (P(("blk", "grp"), None), P(("blk", "grp"), None), P(), P())
    out_specs = (P(("blk", "grp")), P(("blk", "grp"), None), P(("blk", "grp"), None))
    return jax.shard_map(
        on_device, mesh=mesh, in_specs=in_specs, out_specs=out_specs, check_vma=False
    )
```

```python
import jax
import jax.numpy as jnp
from jax import lax
from jax.experimental import pallas as pl
from jax.experimental.pallas import tpu as pltpu
from jax.sharding import PartitionSpec as P

MESH = pl.DeviceIdType.MESH
F32 = jnp.float32
BF16 = jnp.bfloat16

ROWS = 128
WIDTH = 1152
BLOCKS = 9
NZ = 32
CHUNKS = 4
CH = ROWS // CHUNKS

OWN, SIB, PREV, NEXT, EDGE = range(5)


def kernel(
    img_ref, txt_ref, ls_ref, bias_ref,
    loss_ref, gimg_ref, gtxt_ref,
    emb, early, ring, late_r, late_y, acc, loss_acc, relay,
    in_sem, ring_s, ring_r, next_s, next_r, prev_s, prev_r, sib_s, sib_r,
    fy_s, fy_r, rs_s, rs_r, ys_s, ys_r,
    scat_s, scat_r, wrap_s, wrap_r, own_s,
):
    blk, grp = lax.axis_index("blk"), lax.axis_index("grp")
    zhi, core = grp // 2, grp % 2
    zlo, xy = blk // 16, blk % 16
    z = zhi * 16 + zlo

    def at_z(zz):
        return {"blk": (zz % 16) * 16 + xy, "grp": (zz // 16) * 2 + core}

    up, down = at_z((z + 1) % NZ), at_z((z + NZ - 1) % NZ)
    side = 1 - 2 * zhi
    after = {"blk": (blk + side + 256) % 256, "grp": grp}
    before = {"blk": (blk - side + 256) % 256, "grp": grp}
    sibling = {"blk": blk, "grp": grp + 1 - 2 * core}
    role = core + zhi - 2 * core * zhi

    at_lo, at_hi = xy == 0, xy == 15
    wrap_next = xy == 15 * (1 - zhi)
    wrap_prev = xy == 15 * zhi
    ends = (15, 0)
    plane = zlo * 16
    beyond = ((plane + 16) % 256, (plane + 255) % 256)
    planes = ((plane + 240) % 256, (plane + 16) % 256)

    def dev_at(b):
        return {"blk": b, "grp": grp}

    half = ROWS // 2
    loads = []
    for h in range(2):
        for src, i in ((img_ref, 0), (txt_ref, 1)):
            r = pl.ds(h * half, half)
            copy = pltpu.make_async_copy(src.at[r], emb.at[i, r], in_sem.at[i, h])
            copy.start()
            loads.append((copy, i, h))

    barrier = pltpu.get_barrier_semaphore()

    def greet(dev):
        pl.semaphore_signal(barrier, inc=1, device_id=dev, device_id_type=MESH)

    for dev in (up, down, after, before, sibling):
        greet(dev)
    count = 7 + 14 * (xy // 15) + 14 * ((15 - xy) // 15)
    for k in range(2):
        is_end = xy == ends[k]

        @pl.when(jnp.logical_not(is_end))
        def _():
            greet(dev_at(plane + ends[k]))

        @pl.when(xy == ends[1 - k])
        def _():
            def one(c, _):
                greet(dev_at(planes[k] + c + k))
                return _

            lax.fori_loop(0, 15, one, 0)

    for copy, i, h in loads:
        copy.wait()
        for c in range(2):
            r = pl.ds(h * half + c * CH, CH)
            x = emb[i, r, :]
            inv = lax.rsqrt(jnp.sum(x * x, axis=1, keepdims=True) + 1e-06)
            early[OWN, i, r, :] = (x * inv).astype(BF16)
    acc[...] = jnp.zeros_like(acc)
    loss_acc[...] = jnp.zeros_like(loss_acc)
    scale = jnp.exp(jnp.full((1, 128), ls_ref[0], F32))
    offset = bias_ref[0]

    pl.semaphore_wait(barrier, count)

    def remote(src, dst, ss, rs, dev):
        return pltpu.make_async_remote_copy(
            src_ref=src, dst_ref=dst, send_sem=ss, recv_sem=rs, device_id=dev, device_id_type=MESH
        )

    def rows(j):
        return pl.ds(j * CH, CH)

    def hop(h, d, j, first=False, last=False):
        if first:
            src = early.at[OWN if j < CHUNKS // 2 else NEXT, d, rows(j)]
        else:
            src = ring.at[h - 1, d, rows(j)]
        dst = late_r.at[d, rows(j)] if last else ring.at[h, d, rows(j)]
        return remote(src, dst, ring_s.at[h, d, j], ring_r.at[h, d, j], up if d == 0 else down)

    def to_before(d, j):
        return remote(
            early.at[OWN, d, rows(j)], early.at[NEXT, d, rows(j)], next_s.at[d, j], next_r.at[d, j], before
        )

    def to_after(d):
        return remote(early.at[OWN, d], early.at[PREV, d], prev_s.at[d], prev_r.at[d], after)

    own_to_sib = remote(early.at[OWN], early.at[SIB], sib_s.at[0], sib_r.at[0], sibling)
    edge_to_sib = remote(early.at[NEXT - role], early.at[EDGE], sib_s.at[1], sib_r.at[1], sibling)

    def unit_of(slot, u):
        return early.at[slot, u // 8, pl.ds(pl.multiple_of((u % 8) * 16, 16), 16)]

    def scatter(k, c):
        return remote(unit_of(OWN, c), relay.at[k], scat_s.at[k, c], scat_r.at[k], dev_at(plane + c))

    def relayed(k, u):
        slot = 2 + zhi if k == 0 else 3 - zhi
        return remote(relay.at[k], unit_of(slot, u), wrap_s.at[k], wrap_r.at[k, u], dev_at(beyond[k]))

    def straight(k):
        slot = 2 + zhi if k == 0 else 3 - zhi
        return remote(
            unit_of(OWN, ends[k]), unit_of(slot, ends[k]), own_s.at[k], wrap_r.at[k, ends[k]], dev_at(beyond[k])
        )

    def wait_units(k, rows_from):
        def one(v, _):
            relayed(k, (v // 4) * 8 + rows_from + v % 4).wait_recv()
            return _

        lax.fori_loop(0, 8, one, 0)

    def on_side(wrapped, fn):
        for k in range(2):
            @pl.when(wrapped & (at_lo if k == 0 else at_hi))
            def _():
                fn(k)

    for j in range(CHUNKS // 2):
        for d in range(2):
            hop(0, d, j, first=True).start()
    for k in range(2):
        @pl.when(xy == ends[k])
        def _():
            straight(k).start()

            def one(c, _):
                scatter(k, c + k).start()
                return _

            lax.fori_loop(0, 15, one, 0)

    @pl.when(jnp.logical_not(wrap_prev))
    def _():
        for j in range(CHUNKS // 2, CHUNKS):
            for d in range(2):
                to_before(d, j).start()

    @pl.when(jnp.logical_not(wrap_next))
    def _():
        for d in range(2):
            to_after(d).start()

    @pl.when(jnp.logical_not(wrap_prev))
    def _():
        for j in range(CHUNKS // 2):
            for d in range(2):
                to_before(d, j).start()

    own_to_sib.start()
    for k in range(2):
        @pl.when(xy != ends[k])
        def _():
            scatter(k, xy).wait_recv()
            relayed(k, xy).start()

    def forward(h, parts=(0, 2, 1, 3), last=False):
        for j in parts:
            for d in range(2):
                hop(h - 1, d, j, first=True).wait_recv()
                hop(h, d, j, last=last).start()

    FRONT, BACK = (0, 1), (2, 3)
    forward(1, FRONT)

    @pl.when(jnp.logical_not(wrap_next))
    def _():
        for j in BACK:
            for d in range(2):
                to_before(d, j).wait_recv()

    on_side(wrap_next, lambda k: wait_units(k, 4))
    for j in BACK:
        for d in range(2):
            hop(0, d, j, first=True).start()

    def unit(i, y, diagonal=None):
        s = lax.dot_general(
            early[OWN, i], y, (((1,), (1,)), ((), ())), preferred_element_type=F32
        )
        u = scale * s + offset
        if diagonal is not None:
            same = lax.broadcasted_iota(jnp.int32, u.shape, 0) == lax.broadcasted_iota(jnp.int32, u.shape, 1)
            flip = jnp.where(same, 1.0 - 2.0 * diagonal, 1.0)
            u = u * flip
        e = jnp.exp(-jnp.abs(u))
        c = scale * (jnp.where(u >= 0, 1.0, e) / (1.0 + e))
        if diagonal is not None:
            c = c * flip
        acc[i] += jnp.dot(c.astype(BF16), y, preferred_element_type=F32)
        if i == 0:
            loss_acc[...] += jnp.maximum(u, 0.0) + jnp.log1p(e)

    def skewed(h, _):
        forward(h, FRONT)
        forward(h - 1, BACK)
        return _

    lax.fori_loop(2, 6, skewed, 0)
    forward(5, BACK)

    own_to_sib.wait_recv()

    @pl.when(jnp.logical_not(wrap_next))
    def _():
        for d in range(2):
            for j in FRONT:
                to_before(d, j).wait_recv()

    @pl.when(jnp.logical_not(wrap_prev))
    def _():
        for d in range(2):
            to_after(d).wait_recv()

    on_side(wrap_next, lambda k: wait_units(k, 0))

    def all_units(k):
        wait_units(k, 0)
        wait_units(k, 4)

    on_side(wrap_prev, all_units)
    edge_to_sib.start()

    def with_unit(p, _):
        diagonal = jnp.where(p == 0, 1.0, 0.0).astype(F32)
        forward(6 + 2 * p)
        unit(0, early[p, 1], diagonal)
        forward(7 + 2 * p)
        unit(1, early[p, 0], diagonal)
        return _

    lax.fori_loop(0, 4, with_unit, 0)
    edge_to_sib.wait_recv()
    forward(14)
    unit(0, early[EDGE, 1])
    forward(15, last=True)
    unit(1, early[EDGE, 0])

    def fwd_y(d, j):
        return remote(
            late_r.at[d, rows(j)], late_y.at[d, rows(j)], fy_s.at[d, j], fy_r.at[d, j],
            after if j < CHUNKS // 2 else before,
        )

    def fwd_rs(d, j):
        return remote(
            late_r.at[d, rows(j)], late_r.at[d, rows(CHUNKS + j)], rs_s.at[d, j], rs_r.at[d, j], sibling
        )

    def fwd_ys(d, j):
        return remote(
            late_y.at[d, rows(j)], late_y.at[d, rows(CHUNKS + j)], ys_s.at[d, j], ys_r.at[d, j], sibling
        )

    chunks = [(d, j) for j in (0, 2, 1, 3) for d in range(2)]
    for d, j in chunks:
        hop(15, d, j, first=True, last=True).wait_recv()
        fwd_y(d, j).start()
        fwd_rs(d, j).start()
    lo, hi = pl.ds(0, ROWS), pl.ds(ROWS, ROWS)
    for i in range(2):
        unit(i, late_r[1 - i, lo])
    for d, j in chunks:
        fwd_y(d, j).wait_recv()
        fwd_ys(d, j).start()
    for d, j in chunks:
        fwd_rs(d, j).wait_recv()
    for i in range(2):
        unit(i, late_r[1 - i, hi])
        unit(i, late_y[1 - i, lo])
    for d, j in chunks:
        fwd_ys(d, j).wait_recv()
    for i in range(2):
        unit(i, late_y[1 - i, hi])

    for dst, i in ((gimg_ref, 0), (gtxt_ref, 1)):
        for c in range(CHUNKS):
            r = pl.ds(c * CH, CH)
            x = emb[i, r, :]
            g = acc[i, r, :]
            inv = lax.rsqrt(jnp.sum(x * x, axis=1, keepdims=True) + 1e-06)
            x = x * inv
            dst[r, :] = (g - x * jnp.sum(x * g, axis=1, keepdims=True)) * inv
    loss_ref[...] = jnp.sum(loss_acc[...].T, axis=0) / (BLOCKS * ROWS)

    def sent(h, _):
        for d in range(2):
            for j in range(CHUNKS):
                hop(h, d, j, first=True).wait_send()
        return _

    lax.fori_loop(0, 15, sent, 0)
    for d, j in chunks:
        hop(15, d, j, first=True, last=True).wait_send()
        fwd_y(d, j).wait_send()
        fwd_rs(d, j).wait_send()
        fwd_ys(d, j).wait_send()

    @pl.when(jnp.logical_not(wrap_prev))
    def _():
        for d, j in chunks:
            to_before(d, j).wait_send()

    @pl.when(jnp.logical_not(wrap_next))
    def _():
        for d in range(2):
            to_after(d).wait_send()

    for k in range(2):
        @pl.when(xy == ends[k])
        def _():
            straight(k).wait_send()

            def one(c, _):
                scatter(k, c + k).wait_send()
                return _

            lax.fori_loop(0, 15, one, 0)

        @pl.when(xy != ends[k])
        def _():
            relayed(k, xy).wait_send()

    own_to_sib.wait_send()
    edge_to_sib.wait_send()


def on_device(image_emb, text_emb, log_scale, bias):
    vmem, smem = pl.BlockSpec(memory_space=pltpu.VMEM), pl.BlockSpec(memory_space=pltpu.SMEM)
    dma = pltpu.SemaphoreType.DMA
    return pl.pallas_call(
        kernel,
        out_shape=(
            jax.ShapeDtypeStruct((ROWS,), F32),
            jax.ShapeDtypeStruct((ROWS, WIDTH), F32),
            jax.ShapeDtypeStruct((ROWS, WIDTH), F32),
        ),
        in_specs=[pl.BlockSpec(memory_space=pl.ANY)] * 2 + [smem, smem],
        out_specs=(vmem, vmem, vmem),
        scratch_shapes=[
            pltpu.VMEM((2, ROWS, WIDTH), F32),
            pltpu.VMEM((5, 2, ROWS, WIDTH), BF16),
            pltpu.VMEM((15, 2, ROWS, WIDTH), BF16),
            pltpu.VMEM((2, 2 * ROWS, WIDTH), BF16),
            pltpu.VMEM((2, 2 * ROWS, WIDTH), BF16),
            pltpu.VMEM((2, ROWS, WIDTH), F32),
            pltpu.VMEM((ROWS, ROWS), F32),
            pltpu.VMEM((2, 16, WIDTH), BF16),
            dma((2, 2)),
            dma((16, 2, CHUNKS)), dma((16, 2, CHUNKS)),
            dma((2, CHUNKS)), dma((2, CHUNKS)),
            dma((2,)), dma((2,)),
            dma((2,)), dma((2,)),
            dma((2, CHUNKS)), dma((2, CHUNKS)),
            dma((2, CHUNKS)), dma((2, CHUNKS)),
            dma((2, CHUNKS)), dma((2, CHUNKS)),
            dma((2, 16)), dma((2,)), dma((2,)), dma((2, 16)), dma((2,)),
        ],
        compiler_params=pltpu.CompilerParams(
            collective_id=0, has_side_effects=True, vmem_limit_bytes=40 * 2**20
        ),
    )(image_emb, text_emb, log_scale, bias)


def solution(mesh):
    in_specs = (P(("blk", "grp"), None), P(("blk", "grp"), None), P(), P())
    out_specs = (P(("blk", "grp")), P(("blk", "grp"), None), P(("blk", "grp"), None))
    return jax.shard_map(
        on_device, mesh=mesh, in_specs=in_specs, out_specs=out_specs, check_vma=False
    )
```

```python
import jax
import jax.numpy as jnp
from jax import lax
from jax.experimental import pallas as pl
from jax.experimental.pallas import tpu as pltpu
from jax.sharding import PartitionSpec as P

MESH = pl.DeviceIdType.MESH
F32 = jnp.float32
BF16 = jnp.bfloat16

ROWS = 128
WIDTH = 1152
BLOCKS = 9
NZ = 32
CHUNKS = 4
CH = ROWS // CHUNKS

OWN, SIB, PREV, NEXT, EDGE, XTRA = range(6)


def kernel(
    img_ref, txt_ref, ls_ref, bias_ref,
    loss_ref, gimg_ref, gtxt_ref,
    emb, early, ring, late_r, late_y, acc, loss_acc, relay,
    in_sem, ring_s, ring_r, next_s, next_r, prev_s, prev_r, sib_s, sib_r,
    fy_s, fy_r, rs_s, rs_r, ys_s, ys_r,
    scat_s, scat_r, wrap_s, wrap_r, own_s, xtra_s, xtra_r,
):
    blk, grp = lax.axis_index("blk"), lax.axis_index("grp")
    zhi, core = grp // 2, grp % 2
    zlo, xy = blk // 16, blk % 16
    z = zhi * 16 + zlo

    def at_z(zz):
        return {"blk": (zz % 16) * 16 + xy, "grp": (zz // 16) * 2 + core}

    up, down = at_z((z + 1) % NZ), at_z((z + NZ - 1) % NZ)
    side = 1 - 2 * zhi
    place = z * 16 + xy

    def at_place(p):
        return {"blk": p % 256, "grp": (p // 256) * 2 + core}

    after, before = at_place((place + side + 512) % 512), at_place((place - side + 512) % 512)
    sibling = {"blk": blk, "grp": grp + 1 - 2 * core}
    role = core + zhi - 2 * core * zhi
    inner = ((place + 1) // 256) * (1 - place // 257)
    outer = (511 - place) // 511 + place // 511

    at_lo, at_hi = xy == 0, xy == 15
    wrap_next = xy == 15 * (1 - zhi)
    wrap_prev = xy == 15 * zhi
    ends = (15, 0)
    plane = z * 16
    beyond = ((plane + 16) % 512, (plane + 511) % 512)
    planes = ((plane + 496) % 512, (plane + 16) % 512)

    half = ROWS // 2
    loads = []
    for h in range(2):
        for src, i in ((img_ref, 0), (txt_ref, 1)):
            r = pl.ds(h * half, half)
            copy = pltpu.make_async_copy(src.at[r], emb.at[i, r], in_sem.at[i, h])
            copy.start()
            loads.append((copy, i, h))

    barrier = pltpu.get_barrier_semaphore()

    def greet(dev):
        pl.semaphore_signal(barrier, inc=1, device_id=dev, device_id_type=MESH)

    for dev in (up, down, after, before, sibling):
        greet(dev)
    count = 7 + 14 * (xy // 15) + 14 * ((15 - xy) // 15)
    for k in range(2):
        is_end = xy == ends[k]

        @pl.when(jnp.logical_not(is_end))
        def _():
            greet(at_place(plane + ends[k]))

        @pl.when(xy == ends[1 - k])
        def _():
            def one(c, _):
                greet(at_place(planes[k] + c + k))
                return _

            lax.fori_loop(0, 15, one, 0)

    for copy, i, h in loads:
        copy.wait()
        for c in range(2):
            r = pl.ds(h * half + c * CH, CH)
            x = emb[i, r, :]
            inv = lax.rsqrt(jnp.sum(x * x, axis=1, keepdims=True) + 1e-06)
            early[OWN, i, r, :] = (x * inv).astype(BF16)
    acc[...] = jnp.zeros_like(acc)
    loss_acc[...] = jnp.zeros_like(loss_acc)
    scale = jnp.exp(jnp.full((1, 128), ls_ref[0], F32))
    offset = bias_ref[0]

    pl.semaphore_wait(barrier, count)

    def remote(src, dst, ss, rs, dev):
        return pltpu.make_async_remote_copy(
            src_ref=src, dst_ref=dst, send_sem=ss, recv_sem=rs, device_id=dev, device_id_type=MESH
        )

    def rows(j):
        return pl.ds(j * CH, CH)

    def hop(h, d, j, first=False, last=False):
        if first:
            src = early.at[OWN if j < CHUNKS // 2 else NEXT, d, rows(j)]
        else:
            src = ring.at[h - 1, d, rows(j)]
        dst = late_r.at[d, rows(j)] if last else ring.at[h, d, rows(j)]
        return remote(src, dst, ring_s.at[h, d, j], ring_r.at[h, d, j], up if d == 0 else down)

    def to_before(d, j):
        return remote(
            early.at[OWN, d, rows(j)], early.at[NEXT, d, rows(j)], next_s.at[d, j], next_r.at[d, j], before
        )

    def to_after(d):
        return remote(early.at[OWN, d], early.at[PREV, d], prev_s.at[d], prev_r.at[d], after)

    own_to_sib = remote(early.at[OWN], early.at[SIB], sib_s.at[0], sib_r.at[0], sibling)
    edge_to_sib = remote(early.at[NEXT - role], early.at[EDGE], sib_s.at[1], sib_r.at[1], sibling)
    xtra_to_sib = remote(early.at[XTRA], early.at[EDGE], sib_s.at[1], sib_r.at[1], sibling)

    def unit_of(slot, u):
        return early.at[slot, u // 8, pl.ds(pl.multiple_of((u % 8) * 16, 16), 16)]

    def scatter(k, c):
        return remote(unit_of(OWN, c), relay.at[k], scat_s.at[k, c], scat_r.at[k], at_place(plane + c))

    here = (2 + zhi, 3 - zhi)
    there = (2 + ((z + 1) % NZ) // 16, 3 - ((z + NZ - 1) % NZ) // 16)

    def relayed(k, u, slot):
        return remote(relay.at[k], unit_of(slot, u), wrap_s.at[k], wrap_r.at[k, u], at_place(beyond[k]))

    def straight(k):
        return remote(
            unit_of(OWN, ends[k]), unit_of(there[k], ends[k]), own_s.at[k], wrap_r.at[k, ends[k]], at_place(beyond[k])
        )

    def wait_units(k, rows_from):
        def one(v, _):
            relayed(k, (v // 4) * 8 + rows_from + v % 4, here[k]).wait_recv()
            return _

        lax.fori_loop(0, 8, one, 0)

    def on_side(wrapped, fn):
        for k in range(2):
            @pl.when(wrapped & (at_lo if k == 0 else at_hi))
            def _():
                fn(k)

    for j in range(CHUNKS // 2):
        for d in range(2):
            hop(0, d, j, first=True).start()
    for k in range(2):
        @pl.when(xy == ends[k])
        def _():
            straight(k).start()

            def one(c, _):
                scatter(k, c + k).start()
                return _

            lax.fori_loop(0, 15, one, 0)

    @pl.when(jnp.logical_not(wrap_prev))
    def _():
        for j in range(CHUNKS // 2, CHUNKS):
            for d in range(2):
                to_before(d, j).start()

    @pl.when(jnp.logical_not(wrap_next))
    def _():
        for d in range(2):
            to_after(d).start()

    @pl.when(jnp.logical_not(wrap_prev))
    def _():
        for j in range(CHUNKS // 2):
            for d in range(2):
                to_before(d, j).start()

    own_to_sib.start()
    for k in range(2):
        @pl.when(xy != ends[k])
        def _():
            scatter(k, xy).wait_recv()
            relayed(k, xy, there[k]).start()

    def forward(h, parts=(0, 2, 1, 3), last=False):
        for j in parts:
            for d in range(2):
                hop(h - 1, d, j, first=True).wait_recv()
                hop(h, d, j, last=last).start()

    def xtra(d, j, src=XTRA, src_row=0):
        return remote(
            early.at[src, d, pl.ds((j + src_row) * CH, CH)], early.at[XTRA, d, rows(j)],
            xtra_s.at[d, j], xtra_r.at[d, j], up if d == 0 else down,
        )

    in_end = at_lo | at_hi
    origin = 31 * (xy // 15)

    def forward_xtra(h):
        for d in range(2):
            @pl.when(in_end & ((z + NZ - h if d == 0 else z + h) % NZ == origin))
            def _():
                for j in range(CHUNKS):
                    xtra(d, j).wait_recv()
                    xtra(d, j).start()

    FRONT, BACK = (0, 1), (2, 3)
    forward(1, FRONT)

    @pl.when(jnp.logical_not(wrap_next))
    def _():
        for j in BACK:
            for d in range(2):
                to_before(d, j).wait_recv()

    on_side(wrap_next, lambda k: wait_units(k, 4))
    for j in BACK:
        for d in range(2):
            hop(0, d, j, first=True).start()

    @pl.when(outer == 1)
    def _():
        for k in range(2):
            @pl.when(at_lo if k == 0 else at_hi)
            def _():
                wait_units(k, 0)
                wait_units(k, 4)

        for j in range(CHUNKS):
            for d in range(2):
                xtra(d, j, PREV if j < CHUNKS // 2 else OWN, CHUNKS // 2 if j < CHUNKS // 2 else 0).start()

    def unit(i, y, diagonal=None):
        s = lax.dot_general(
            early[OWN, i], y, (((1,), (1,)), ((), ())), preferred_element_type=F32
        )
        u = scale * s + offset
        if diagonal is not None:
            same = lax.broadcasted_iota(jnp.int32, u.shape, 0) == lax.broadcasted_iota(jnp.int32, u.shape, 1)
            flip = jnp.where(same, 1.0 - 2.0 * diagonal, 1.0)
            u = u * flip
        e = jnp.exp(-jnp.abs(u))
        c = scale * (jnp.where(u >= 0, 1.0, e) / (1.0 + e))
        if diagonal is not None:
            c = c * flip
        acc[i] += jnp.dot(c.astype(BF16), y, preferred_element_type=F32)
        if i == 0:
            loss_acc[...] += jnp.maximum(u, 0.0) + jnp.log1p(e)

    def skewed(h, _):
        forward(h, FRONT)
        forward(h - 1, BACK)
        forward_xtra(h - 1)
        return _

    lax.fori_loop(2, 6, skewed, 0)
    forward(5, BACK)
    forward_xtra(5)

    own_to_sib.wait_recv()

    @pl.when(jnp.logical_not(wrap_next))
    def _():
        for d in range(2):
            for j in FRONT:
                to_before(d, j).wait_recv()

    @pl.when(jnp.logical_not(wrap_prev))
    def _():
        for d in range(2):
            to_after(d).wait_recv()

    on_side(wrap_next, lambda k: wait_units(k, 0))

    def all_units(k):
        wait_units(k, 0)
        wait_units(k, 4)

    on_side(wrap_prev & (outer == 0), all_units)

    @pl.when(inner * (1 - role) == 0)
    def _():
        edge_to_sib.start()

    def with_unit(p, carry):
        diagonal = jnp.where(p == 0, 1.0, 0.0).astype(F32)
        used = inner * (p // 3) == 0
        for i in range(2):
            forward(6 + 2 * p + i)
            forward_xtra(6 + 2 * p + i)

            @pl.when(used)
            def _():
                unit(i, early[p, 1 - i], diagonal)
        return carry

    lax.fori_loop(0, 4, with_unit, 0)
    edge_early = inner * role == 0

    @pl.when(edge_early)
    def _():
        edge_to_sib.wait_recv()

    for i in range(2):
        forward(14 + i, last=i == 1)
        forward_xtra(14 + i)

        @pl.when(edge_early)
        def _():
            unit(i, early[EDGE, 1 - i])

    def part_rows(j):
        return pl.ds(pl.multiple_of(j * CH, CH), CH)

    def fwd_y(d, j):
        if j < CHUNKS // 2:
            src, dst, dev = j, j + 2 * inner, after
        else:
            src, dst, dev = j - 2 * outer, j - 2 * outer, before
        return remote(
            late_r.at[d, part_rows(src)], late_y.at[d, part_rows(dst)], fy_s.at[d, j], fy_r.at[d, dst], dev
        )

    def got_y(d, j):
        return remote(late_r.at[d, rows(j)], late_y.at[d, rows(j)], fy_s.at[d, j], fy_r.at[d, j], after)

    def fwd_rs(d, j, other=None):
        src = late_r.at[d, rows(j)] if other is None else early.at[other, d, rows(j)]
        return remote(src, late_r.at[d, rows(CHUNKS + j)], rs_s.at[d, j], rs_r.at[d, j], sibling)

    def fwd_ys(d, j, other=None):
        src = late_y.at[d, rows(j)] if other is None else early.at[other, d, rows(j)]
        return remote(src, late_y.at[d, rows(CHUNKS + j)], ys_s.at[d, j], ys_r.at[d, j], sibling)

    def either(copy, other, which):
        @pl.when(which)
        def _():
            copy(other).start()

        @pl.when(jnp.logical_not(which))
        def _():
            copy(None).start()

    outer_first, inner_second = outer * (1 - role) == 1, inner * role == 1
    chunks = [(d, j) for j in (0, 2, 1, 3) for d in range(2)]
    for d, j in chunks:
        hop(15, d, j, first=True, last=True).wait_recv()
        fwd_y(d, j).start()
        if j < CHUNKS // 2:
            fwd_rs(d, j).start()
        else:
            either(lambda other: fwd_rs(d, j, other), PREV, outer_first)

    @pl.when(inner == 1)
    def _():
        for d, j in chunks:
            xtra(d, j).wait_recv()

        @pl.when(role == 0)
        def _():
            xtra_to_sib.start()

        for i in range(2):
            unit(i, early[XTRA, 1 - i])

    lo, hi = pl.ds(0, ROWS), pl.ds(ROWS, ROWS)
    for i in range(2):
        unit(i, late_r[1 - i, lo])
    for d, j in chunks:
        got_y(d, j).wait_recv()
        if j < CHUNKS // 2:
            either(lambda other: fwd_ys(d, j, other), PREV, outer_first)
        else:
            either(lambda other: fwd_ys(d, j, other), XTRA, inner_second)
    for d, j in chunks:
        fwd_rs(d, j).wait_recv()
    for i in range(2):
        unit(i, late_r[1 - i, hi])
        unit(i, late_y[1 - i, lo])

    @pl.when(inner * role == 1)
    def _():
        xtra_to_sib.wait_recv()
        for i in range(2):
            unit(i, early[EDGE, 1 - i])

    for d, j in chunks:
        fwd_ys(d, j).wait_recv()
    for i in range(2):
        unit(i, late_y[1 - i, hi])

    for dst, i in ((gimg_ref, 0), (gtxt_ref, 1)):
        for c in range(CHUNKS):
            r = pl.ds(c * CH, CH)
            x = emb[i, r, :]
            g = acc[i, r, :]
            inv = lax.rsqrt(jnp.sum(x * x, axis=1, keepdims=True) + 1e-06)
            x = x * inv
            dst[r, :] = (g - x * jnp.sum(x * g, axis=1, keepdims=True)) * inv
    loss_ref[...] = jnp.sum(loss_acc[...].T, axis=0) / (BLOCKS * ROWS)

    def sent(h, _):
        for d in range(2):
            for j in range(CHUNKS):
                hop(h, d, j, first=True).wait_send()
        return _

    lax.fori_loop(0, 15, sent, 0)
    for d, j in chunks:
        hop(15, d, j, first=True, last=True).wait_send()
        fwd_y(d, j).wait_send()
        fwd_rs(d, j).wait_send()
        fwd_ys(d, j).wait_send()

    @pl.when(jnp.logical_not(wrap_prev))
    def _():
        for d, j in chunks:
            to_before(d, j).wait_send()

    @pl.when(jnp.logical_not(wrap_next))
    def _():
        for d in range(2):
            to_after(d).wait_send()

    for k in range(2):
        @pl.when(xy == ends[k])
        def _():
            straight(k).wait_send()

            def one(c, _):
                scatter(k, c + k).wait_send()
                return _

            lax.fori_loop(0, 15, one, 0)

        @pl.when(xy != ends[k])
        def _():
            relayed(k, xy, there[k]).wait_send()

    @pl.when(outer == 1)
    def _():
        for d, j in chunks:
            xtra(d, j).wait_send()

    for d in range(2):
        gone = (z + NZ - origin if d == 0 else origin + NZ - z) % NZ

        @pl.when(in_end & (gone >= 1) & (gone <= 15))
        def _():
            for j in range(CHUNKS):
                xtra(d, j).wait_send()

    own_to_sib.wait_send()
    edge_to_sib.wait_send()


def on_device(image_emb, text_emb, log_scale, bias):
    vmem, smem = pl.BlockSpec(memory_space=pltpu.VMEM), pl.BlockSpec(memory_space=pltpu.SMEM)
    dma = pltpu.SemaphoreType.DMA
    return pl.pallas_call(
        kernel,
        out_shape=(
            jax.ShapeDtypeStruct((ROWS,), F32),
            jax.ShapeDtypeStruct((ROWS, WIDTH), F32),
            jax.ShapeDtypeStruct((ROWS, WIDTH), F32),
        ),
        in_specs=[pl.BlockSpec(memory_space=pl.ANY)] * 2 + [smem, smem],
        out_specs=(vmem, vmem, vmem),
        scratch_shapes=[
            pltpu.VMEM((2, ROWS, WIDTH), F32),
            pltpu.VMEM((6, 2, ROWS, WIDTH), BF16),
            pltpu.VMEM((15, 2, ROWS, WIDTH), BF16),
            pltpu.VMEM((2, 2 * ROWS, WIDTH), BF16),
            pltpu.VMEM((2, 2 * ROWS, WIDTH), BF16),
            pltpu.VMEM((2, ROWS, WIDTH), F32),
            pltpu.VMEM((ROWS, ROWS), F32),
            pltpu.VMEM((2, 16, WIDTH), BF16),
            dma((2, 2)),
            dma((16, 2, CHUNKS)), dma((16, 2, CHUNKS)),
            dma((2, CHUNKS)), dma((2, CHUNKS)),
            dma((2,)), dma((2,)),
            dma((2,)), dma((2,)),
            dma((2, CHUNKS)), dma((2, CHUNKS)),
            dma((2, CHUNKS)), dma((2, CHUNKS)),
            dma((2, CHUNKS)), dma((2, CHUNKS)),
            dma((2, 16)), dma((2,)), dma((2,)), dma((2, 16)), dma((2,)), dma((2, CHUNKS)), dma((2, CHUNKS)),
        ],
        compiler_params=pltpu.CompilerParams(
            collective_id=0, has_side_effects=True, vmem_limit_bytes=60 * 2**20
        ),
    )(image_emb, text_emb, log_scale, bias)


def solution(mesh):
    in_specs = (P(("blk", "grp"), None), P(("blk", "grp"), None), P(), P())
    out_specs = (P(("blk", "grp")), P(("blk", "grp"), None), P(("blk", "grp"), None))
    return jax.shard_map(
        on_device, mesh=mesh, in_specs=in_specs, out_specs=out_specs, check_vma=False
    )
```

```python
import jax
import jax.numpy as jnp
from jax import lax
from jax.experimental import pallas as pl
from jax.experimental.pallas import tpu as pltpu
from jax.sharding import PartitionSpec as P

MESH = pl.DeviceIdType.MESH
F32 = jnp.float32
BF16 = jnp.bfloat16

ROWS = 128
WIDTH = 1152
BLOCKS = 9
NZ = 32
CHUNKS = 4
CH = ROWS // CHUNKS

OWN, SIB, PREV, NEXT, EDGE, XTRA = range(6)


def kernel(
    img_ref, txt_ref, ls_ref, bias_ref,
    loss_ref, gimg_ref, gtxt_ref,
    emb, early, ring, late_r, late_y, acc, loss_acc, relay, xbuf,
    in_sem, ring_s, ring_r, next_s, next_r, prev_s, prev_r, sib_s, sib_r,
    fy_s, fy_r, rs_s, rs_r, ys_s, ys_r,
    scat_s, scat_r, wrap_s, wrap_r, own_s, flow_s, flow_r, drop_s, xtra_r,
):
    blk, grp = lax.axis_index("blk"), lax.axis_index("grp")
    zhi, core = grp // 2, grp % 2
    zlo, xy = blk // 16, blk % 16
    z = zhi * 16 + zlo

    def at_z(zz):
        return {"blk": (zz % 16) * 16 + xy, "grp": (zz // 16) * 2 + core}

    up, down = at_z((z + 1) % NZ), at_z((z + NZ - 1) % NZ)
    side = 1 - 2 * zhi
    place = z * 16 + xy

    def at_place(p):
        return {"blk": p % 256, "grp": (p // 256) * 2 + core}

    after, before = at_place((place + side + 512) % 512), at_place((place - side + 512) % 512)
    sibling = {"blk": blk, "grp": grp + 1 - 2 * core}
    role = core + zhi - 2 * core * zhi
    inner = ((place + 1) // 256) * (1 - place // 257)
    outer = (511 - place) // 511 + place // 511
    carrier = (xy % 8) // 4
    mid = ((z + 1) // 16) * (1 - z // 17)
    itself = inner * (1 - zhi)
    dropping = carrier * mid * (1 - itself) == 1
    gone = (z, NZ - 1 - z)

    at_lo, at_hi = xy == 0, xy == 15
    wrap_next = xy == 15 * (1 - zhi)
    wrap_prev = xy == 15 * zhi
    ends = (15, 0)
    plane = z * 16
    beyond = ((plane + 16) % 512, (plane + 511) % 512)
    planes = ((plane + 496) % 512, (plane + 16) % 512)

    half = ROWS // 2
    loads = []
    for h in range(2):
        for src, i in ((img_ref, 0), (txt_ref, 1)):
            r = pl.ds(h * half, half)
            copy = pltpu.make_async_copy(src.at[r], emb.at[i, r], in_sem.at[i, h])
            copy.start()
            loads.append((copy, i, h))

    barrier = pltpu.get_barrier_semaphore()

    def greet(dev):
        pl.semaphore_signal(barrier, inc=1, device_id=dev, device_id_type=MESH)

    for dev in (up, down, after, before, sibling):
        greet(dev)
    count = 7 + 14 * (xy // 15) + 14 * ((15 - xy) // 15) + carrier * mid * (1 - itself)
    for k in range(2):
        is_end = xy == ends[k]

        @pl.when(jnp.logical_not(is_end))
        def _():
            greet(at_place(plane + ends[k]))

        @pl.when(xy == ends[1 - k])
        def _():
            def one(c, _):
                greet(at_place(planes[k] + c + k))
                return _

            lax.fori_loop(0, 15, one, 0)

    @pl.when(inner == 1)
    def _():
        def one(v, _):
            greet(at_place(plane + (v // 4) * 8 + 4 + v % 4))
            return _

        lax.fori_loop(0, 7 + zhi, one, 0)

    for copy, i, h in loads:
        copy.wait()
        for c in range(2):
            r = pl.ds(h * half + c * CH, CH)
            x = emb[i, r, :]
            inv = lax.rsqrt(jnp.sum(x * x, axis=1, keepdims=True) + 1e-06)
            early[OWN, i, r, :] = (x * inv).astype(BF16)
    acc[...] = jnp.zeros_like(acc)
    loss_acc[...] = jnp.zeros_like(loss_acc)
    scale = jnp.exp(jnp.full((1, 128), ls_ref[0], F32))
    offset = bias_ref[0]

    pl.semaphore_wait(barrier, count)

    def remote(src, dst, ss, rs, dev):
        return pltpu.make_async_remote_copy(
            src_ref=src, dst_ref=dst, send_sem=ss, recv_sem=rs, device_id=dev, device_id_type=MESH
        )

    def rows(j):
        return pl.ds(j * CH, CH)

    def hop(h, d, j, first=False, last=False):
        if first:
            src = early.at[OWN if j < CHUNKS // 2 else NEXT, d, rows(j)]
        else:
            src = ring.at[h - 1, d, rows(j)]
        dst = late_r.at[d, rows(j)] if last else ring.at[h, d, rows(j)]
        return remote(src, dst, ring_s.at[h, d, j], ring_r.at[h, d, j], up if d == 0 else down)

    def to_before(d, j):
        return remote(
            early.at[OWN, d, rows(j)], early.at[NEXT, d, rows(j)], next_s.at[d, j], next_r.at[d, j], before
        )

    def to_after(d):
        return remote(early.at[OWN, d], early.at[PREV, d], prev_s.at[d], prev_r.at[d], after)

    own_to_sib = remote(early.at[OWN], early.at[SIB], sib_s.at[0], sib_r.at[0], sibling)
    edge_to_sib = remote(early.at[NEXT - role], early.at[EDGE], sib_s.at[1], sib_r.at[1], sibling)
    xtra_to_sib = remote(early.at[XTRA], early.at[EDGE], sib_s.at[1], sib_r.at[1], sibling)

    def unit_of(slot, u):
        return early.at[slot, u // 8, pl.ds(pl.multiple_of((u % 8) * 16, 16), 16)]

    def scatter(k, c):
        return remote(unit_of(OWN, c), relay.at[k], scat_s.at[k, c], scat_r.at[k], at_place(plane + c))

    here = (2 + zhi, 3 - zhi)
    there = (2 + ((z + 1) % NZ) // 16, 3 - ((z + NZ - 1) % NZ) // 16)

    def relayed(k, u, slot):
        return remote(relay.at[k], unit_of(slot, u), wrap_s.at[k], wrap_r.at[k, u], at_place(beyond[k]))

    def straight(k):
        return remote(
            unit_of(OWN, ends[k]), unit_of(there[k], ends[k]), own_s.at[k], wrap_r.at[k, ends[k]], at_place(beyond[k])
        )

    def wait_units(k, rows_from):
        def one(v, _):
            relayed(k, (v // 4) * 8 + rows_from + v % 4, here[k]).wait_recv()
            return _

        lax.fori_loop(0, 8, one, 0)

    def on_side(wrapped, fn):
        for k in range(2):
            @pl.when(wrapped & (at_lo if k == 0 else at_hi))
            def _():
                fn(k)

    for j in range(CHUNKS // 2):
        for d in range(2):
            hop(0, d, j, first=True).start()
    for k in range(2):
        @pl.when(xy == ends[k])
        def _():
            straight(k).start()

            def one(c, _):
                scatter(k, c + k).start()
                return _

            lax.fori_loop(0, 15, one, 0)

    @pl.when(jnp.logical_not(wrap_prev))
    def _():
        for j in range(CHUNKS // 2, CHUNKS):
            for d in range(2):
                to_before(d, j).start()

    @pl.when(jnp.logical_not(wrap_next))
    def _():
        for d in range(2):
            to_after(d).start()

    @pl.when(jnp.logical_not(wrap_prev))
    def _():
        for j in range(CHUNKS // 2):
            for d in range(2):
                to_before(d, j).start()

    own_to_sib.start()

    def flow(d, src=None):
        return remote(
            xbuf.at[d] if src is None else src, xbuf.at[d], flow_s.at[d], flow_r.at[d], up if d == 0 else down
        )

    for k in range(2):
        @pl.when(xy != ends[k])
        def _():
            scatter(k, xy).wait_recv()
            relayed(k, xy, there[k]).start()

            @pl.when((carrier == 1) & (gone[1 - k] == 0))
            def _():
                flow(1 - k, relay.at[k]).start()

    @pl.when(place == 511)
    def _():
        flow(1, unit_of(OWN, 15)).start()

    def forward(h, parts=(0, 2, 1, 3), last=False):
        for j in parts:
            for d in range(2):
                hop(h - 1, d, j, first=True).wait_recv()
                hop(h, d, j, last=last).start()

    def forward_xtra(h):
        for d in range(2):
            @pl.when((carrier == 1) & (gone[d] == h))
            def _():
                flow(d).wait_recv()
                flow(d).start()

    def xtra_rows(d, v):
        return pl.ds(pl.multiple_of((d + zhi - 2 * d * zhi) * half + (v % 4) * 16, 16), 16)

    def drop(d, v):
        return remote(
            xbuf.at[d], early.at[XTRA, v // 4, xtra_rows(d, v)], drop_s.at[d], xtra_r.at[d, v], at_place(z + 240)
        )

    mine = (xy // 8) * 4 + xy % 4

    FRONT, BACK = (0, 1), (2, 3)
    forward(1, FRONT)

    @pl.when(jnp.logical_not(wrap_next))
    def _():
        for j in BACK:
            for d in range(2):
                to_before(d, j).wait_recv()

    on_side(wrap_next, lambda k: wait_units(k, 4))
    for j in BACK:
        for d in range(2):
            hop(0, d, j, first=True).start()

    def unit(i, y, diagonal=None):
        s = lax.dot_general(
            early[OWN, i], y, (((1,), (1,)), ((), ())), preferred_element_type=F32
        )
        u = scale * s + offset
        if diagonal is not None:
            same = lax.broadcasted_iota(jnp.int32, u.shape, 0) == lax.broadcasted_iota(jnp.int32, u.shape, 1)
            flip = jnp.where(same, 1.0 - 2.0 * diagonal, 1.0)
            u = u * flip
        e = jnp.exp(-jnp.abs(u))
        c = scale * (jnp.where(u >= 0, 1.0, e) / (1.0 + e))
        if diagonal is not None:
            c = c * flip
        acc[i] += jnp.dot(c.astype(BF16), y, preferred_element_type=F32)
        if i == 0:
            loss_acc[...] += jnp.maximum(u, 0.0) + jnp.log1p(e)

    def skewed(h, _):
        forward(h, FRONT)
        forward(h - 1, BACK)
        forward_xtra(h - 1)
        return _

    lax.fori_loop(2, 6, skewed, 0)
    forward(5, BACK)
    forward_xtra(5)

    own_to_sib.wait_recv()

    @pl.when(jnp.logical_not(wrap_next))
    def _():
        for d in range(2):
            for j in FRONT:
                to_before(d, j).wait_recv()

    @pl.when(jnp.logical_not(wrap_prev))
    def _():
        for d in range(2):
            to_after(d).wait_recv()

    on_side(wrap_next, lambda k: wait_units(k, 0))

    def all_units(k):
        wait_units(k, 0)
        wait_units(k, 4)

    on_side(wrap_prev, all_units)

    @pl.when(inner * (1 - role) == 0)
    def _():
        edge_to_sib.start()

    def with_unit(p, carry):
        diagonal = jnp.where(p == 0, 1.0, 0.0).astype(F32)
        used = inner * (p // 3) == 0
        for i in range(2):
            forward(6 + 2 * p + i)
            forward_xtra(6 + 2 * p + i)

            @pl.when(used)
            def _():
                unit(i, early[p, 1 - i], diagonal)
        return carry

    lax.fori_loop(0, 4, with_unit, 0)
    edge_early = inner * role == 0

    @pl.when(edge_early)
    def _():
        edge_to_sib.wait_recv()

    for i in range(2):
        forward(14 + i, last=i == 1)
        forward_xtra(14 + i)

        @pl.when(edge_early)
        def _():
            unit(i, early[EDGE, 1 - i])

    def part_rows(j):
        return pl.ds(pl.multiple_of(j * CH, CH), CH)

    def fwd_y(d, j):
        if j < CHUNKS // 2:
            src, dst, dev = j, j + 2 * inner, after
        else:
            src, dst, dev = j - 2 * outer, j - 2 * outer, before
        return remote(
            late_r.at[d, part_rows(src)], late_y.at[d, part_rows(dst)], fy_s.at[d, j], fy_r.at[d, dst], dev
        )

    def got_y(d, j):
        return remote(late_r.at[d, rows(j)], late_y.at[d, rows(j)], fy_s.at[d, j], fy_r.at[d, j], after)

    def fwd_rs(d, j, other=None):
        src = late_r.at[d, rows(j)] if other is None else early.at[other, d, rows(j)]
        return remote(src, late_r.at[d, rows(CHUNKS + j)], rs_s.at[d, j], rs_r.at[d, j], sibling)

    def fwd_ys(d, j, other=None):
        src = late_y.at[d, rows(j)] if other is None else early.at[other, d, rows(j)]
        return remote(src, late_y.at[d, rows(CHUNKS + j)], ys_s.at[d, j], ys_r.at[d, j], sibling)

    def either(copy, other, which):
        @pl.when(which)
        def _():
            copy(other).start()

        @pl.when(jnp.logical_not(which))
        def _():
            copy(None).start()

    outer_first, inner_second = outer * (1 - role) == 1, inner * role == 1
    chunks = [(d, j) for j in (0, 2, 1, 3) for d in range(2)]
    for d, j in chunks:
        hop(15, d, j, first=True, last=True).wait_recv()
        fwd_y(d, j).start()
        if j < CHUNKS // 2:
            fwd_rs(d, j).start()
        else:
            either(lambda other: fwd_rs(d, j, other), PREV, outer_first)

    for d in range(2):
        @pl.when(carrier * mid == 1)
        def _():
            @pl.when(gone[d] == 16)
            def _():
                flow(d).wait_recv()

        @pl.when(dropping)
        def _():
            drop(d, mine).start()

        @pl.when(itself == 1)
        def _():
            early[XTRA, 1, pl.ds(d * half + 48, 16), :] = xbuf[d]

    @pl.when(inner == 1)
    def _():
        for d in range(2):
            def one(v, _):
                drop(d, v).wait_recv()
                return _

            lax.fori_loop(0, 7 + zhi, one, 0)

        @pl.when(role == 0)
        def _():
            xtra_to_sib.start()

        for i in range(2):
            unit(i, early[XTRA, 1 - i])

    lo, hi = pl.ds(0, ROWS), pl.ds(ROWS, ROWS)
    for i in range(2):
        unit(i, late_r[1 - i, lo])
    for d, j in chunks:
        got_y(d, j).wait_recv()
        if j < CHUNKS // 2:
            either(lambda other: fwd_ys(d, j, other), PREV, outer_first)
        else:
            either(lambda other: fwd_ys(d, j, other), XTRA, inner_second)
    for d, j in chunks:
        fwd_rs(d, j).wait_recv()
    for i in range(2):
        unit(i, late_r[1 - i, hi])
        unit(i, late_y[1 - i, lo])

    @pl.when(inner * role == 1)
    def _():
        xtra_to_sib.wait_recv()
        for i in range(2):
            unit(i, early[EDGE, 1 - i])

    for d, j in chunks:
        fwd_ys(d, j).wait_recv()
    for i in range(2):
        unit(i, late_y[1 - i, hi])

    for dst, i in ((gimg_ref, 0), (gtxt_ref, 1)):
        for c in range(CHUNKS):
            r = pl.ds(c * CH, CH)
            x = emb[i, r, :]
            g = acc[i, r, :]
            inv = lax.rsqrt(jnp.sum(x * x, axis=1, keepdims=True) + 1e-06)
            x = x * inv
            dst[r, :] = (g - x * jnp.sum(x * g, axis=1, keepdims=True)) * inv
    loss_ref[...] = jnp.sum(loss_acc[...].T, axis=0) / (BLOCKS * ROWS)

    def sent(h, _):
        for d in range(2):
            for j in range(CHUNKS):
                hop(h, d, j, first=True).wait_send()
        return _

    lax.fori_loop(0, 15, sent, 0)
    for d, j in chunks:
        hop(15, d, j, first=True, last=True).wait_send()
        fwd_y(d, j).wait_send()
        fwd_rs(d, j).wait_send()
        fwd_ys(d, j).wait_send()

    @pl.when(jnp.logical_not(wrap_prev))
    def _():
        for d, j in chunks:
            to_before(d, j).wait_send()

    @pl.when(jnp.logical_not(wrap_next))
    def _():
        for d in range(2):
            to_after(d).wait_send()

    for k in range(2):
        @pl.when(xy == ends[k])
        def _():
            straight(k).wait_send()

            def one(c, _):
                scatter(k, c + k).wait_send()
                return _

            lax.fori_loop(0, 15, one, 0)

        @pl.when(xy != ends[k])
        def _():
            relayed(k, xy, there[k]).wait_send()

    for d in range(2):
        @pl.when((carrier == 1) & (gone[d] <= 15))
        def _():
            flow(d).wait_send()

        @pl.when(dropping)
        def _():
            drop(d, mine).wait_send()

    own_to_sib.wait_send()
    edge_to_sib.wait_send()


def on_device(image_emb, text_emb, log_scale, bias):
    vmem, smem = pl.BlockSpec(memory_space=pltpu.VMEM), pl.BlockSpec(memory_space=pltpu.SMEM)
    dma = pltpu.SemaphoreType.DMA
    return pl.pallas_call(
        kernel,
        out_shape=(
            jax.ShapeDtypeStruct((ROWS,), F32),
            jax.ShapeDtypeStruct((ROWS, WIDTH), F32),
            jax.ShapeDtypeStruct((ROWS, WIDTH), F32),
        ),
        in_specs=[pl.BlockSpec(memory_space=pl.ANY)] * 2 + [smem, smem],
        out_specs=(vmem, vmem, vmem),
        scratch_shapes=[
            pltpu.VMEM((2, ROWS, WIDTH), F32),
            pltpu.VMEM((6, 2, ROWS, WIDTH), BF16),
            pltpu.VMEM((15, 2, ROWS, WIDTH), BF16),
            pltpu.VMEM((2, 2 * ROWS, WIDTH), BF16),
            pltpu.VMEM((2, 2 * ROWS, WIDTH), BF16),
            pltpu.VMEM((2, ROWS, WIDTH), F32),
            pltpu.VMEM((ROWS, ROWS), F32),
            pltpu.VMEM((2, 16, WIDTH), BF16),
            pltpu.VMEM((2, 16, WIDTH), BF16),
            dma((2, 2)),
            dma((16, 2, CHUNKS)), dma((16, 2, CHUNKS)),
            dma((2, CHUNKS)), dma((2, CHUNKS)),
            dma((2,)), dma((2,)),
            dma((2,)), dma((2,)),
            dma((2, CHUNKS)), dma((2, CHUNKS)),
            dma((2, CHUNKS)), dma((2, CHUNKS)),
            dma((2, CHUNKS)), dma((2, CHUNKS)),
            dma((2, 16)), dma((2,)), dma((2,)), dma((2, 16)), dma((2,)),
            dma((2,)), dma((2,)), dma((2,)), dma((2, 8)),
        ],
        compiler_params=pltpu.CompilerParams(
            collective_id=0, has_side_effects=True, vmem_limit_bytes=55050240
        ),
    )(image_emb, text_emb, log_scale, bias)


def solution(mesh):
    in_specs = (P(("blk", "grp"), None), P(("blk", "grp"), None), P(), P())
    out_specs = (P(("blk", "grp")), P(("blk", "grp"), None), P(("blk", "grp"), None))
    return jax.shard_map(
        on_device, mesh=mesh, in_specs=in_specs, out_specs=out_specs, check_vma=False
    )
```

```python
import jax
import jax.numpy as jnp
from jax import lax
from jax.experimental import pallas as pl
from jax.experimental.pallas import tpu as pltpu
from jax.sharding import PartitionSpec as P

MESH = pl.DeviceIdType.MESH
F32 = jnp.float32
BF16 = jnp.bfloat16

ROWS = 128
WIDTH = 1152
BLOCKS = 9
NZ = 32
CHUNKS = 4
CH = ROWS // CHUNKS

OWN, SIB, PREV, NEXT, EDGE, XTRA = range(6)


def kernel(
    img_ref, txt_ref, ls_ref, bias_ref,
    loss_ref, gimg_ref, gtxt_ref,
    emb, early, ring, late_r, late_y, acc, loss_acc, relay, xbuf,
    in_sem, ring_s, ring_r, next_s, next_r, prev_s, prev_r, sib_s, sib_r,
    fy_s, fy_r, rs_s, rs_r, ys_s, ys_r,
    scat_s, scat_r, wrap_s, wrap_r, flow_s, flow_r, drop_s, xtra_r,
):
    blk, grp = lax.axis_index("blk"), lax.axis_index("grp")
    zhi, core = grp // 2, grp % 2
    zlo, xy = blk // 16, blk % 16
    z = zhi * 16 + zlo

    def at_z(zz):
        return {"blk": (zz % 16) * 16 + xy, "grp": (zz // 16) * 2 + core}

    up, down = at_z((z + 1) % NZ), at_z((z + NZ - 1) % NZ)
    side = 1 - 2 * zhi
    place = z * 16 + xy

    def at_place(p):
        return {"blk": p % 256, "grp": (p // 256) * 2 + core}

    after, before = at_place((place + side + 512) % 512), at_place((place - side + 512) % 512)
    sibling = {"blk": blk, "grp": grp + 1 - 2 * core}
    role = core + zhi - 2 * core * zhi
    inner = ((place + 1) // 256) * (1 - place // 257)
    outer = (511 - place) // 511 + place // 511
    mover = ((xy + 4) // 8) % 2
    carrier = mover * ((xy % 4) // 2)
    mid = ((z + 1) // 16) * (1 - z // 17)
    dropping = carrier * mid == 1
    gone = (z, NZ - 1 - z)

    at_lo, at_hi = xy == 0, xy == 15
    wrap_next = xy == 15 * (1 - zhi)
    wrap_prev = xy == 15 * zhi
    ends = (15, 0)
    plane = z * 16
    beyond = ((plane + 16) % 512, (plane + 511) % 512)
    planes = ((plane + 496) % 512, (plane + 16) % 512)

    half = ROWS // 2
    loads = []
    for h in range(2):
        for src, i in ((img_ref, 0), (txt_ref, 1)):
            r = pl.ds(h * half, half)
            copy = pltpu.make_async_copy(src.at[r], emb.at[i, r], in_sem.at[i, h])
            copy.start()
            loads.append((copy, i, h))

    barrier = pltpu.get_barrier_semaphore()

    def greet(dev):
        pl.semaphore_signal(barrier, inc=1, device_id=dev, device_id_type=MESH)

    for dev in (up, down, after, before, sibling):
        greet(dev)
    count = 5 + 8 * (xy // 15) + 8 * ((15 - xy) // 15) + 2 * mover + carrier * mid
    for k in range(2):
        @pl.when(mover == 1)
        def _():
            greet(at_place(plane + ends[k]))

        @pl.when(xy == ends[1 - k])
        def _():
            def one(c, _):
                greet(at_place((planes[k] + 4 + c) % 512))
                return _

            lax.fori_loop(0, 8, one, 0)

    @pl.when(inner == 1)
    def _():
        def one(v, _):
            greet(at_place(plane + (v // 2) * 4 + 6 + v % 2))
            return _

        lax.fori_loop(0, 4, one, 0)

    for copy, i, h in loads:
        copy.wait()
        for c in range(2):
            r = pl.ds(h * half + c * CH, CH)
            x = emb[i, r, :]
            inv = lax.rsqrt(jnp.sum(x * x, axis=1, keepdims=True) + 1e-06)
            early[OWN, i, r, :] = (x * inv).astype(BF16)
    acc[...] = jnp.zeros_like(acc)
    loss_acc[...] = jnp.zeros_like(loss_acc)
    scale = jnp.exp(jnp.full((1, 128), ls_ref[0], F32))
    offset = bias_ref[0]

    pl.semaphore_wait(barrier, count)

    def remote(src, dst, ss, rs, dev):
        return pltpu.make_async_remote_copy(
            src_ref=src, dst_ref=dst, send_sem=ss, recv_sem=rs, device_id=dev, device_id_type=MESH
        )

    def rows(j):
        return pl.ds(j * CH, CH)

    def hop(h, d, j, first=False, last=False):
        if first:
            src = early.at[OWN if j < CHUNKS // 2 else NEXT, d, rows(j)]
        else:
            src = ring.at[h - 1, d, rows(j)]
        dst = late_r.at[d, rows(j)] if last else ring.at[h, d, rows(j)]
        return remote(src, dst, ring_s.at[h, d, j], ring_r.at[h, d, j], up if d == 0 else down)

    def to_before(d, j):
        return remote(
            early.at[OWN, d, rows(j)], early.at[NEXT, d, rows(j)], next_s.at[d, j], next_r.at[d, j], before
        )

    def to_after(d):
        return remote(early.at[OWN, d], early.at[PREV, d], prev_s.at[d], prev_r.at[d], after)

    own_to_sib = remote(early.at[OWN], early.at[SIB], sib_s.at[0], sib_r.at[0], sibling)
    edge_to_sib = remote(early.at[NEXT - role], early.at[EDGE], sib_s.at[1], sib_r.at[1], sibling)
    xtra_to_sib = remote(early.at[XTRA], early.at[EDGE], sib_s.at[1], sib_r.at[1], sibling)

    def unit_of(slot, u):
        return early.at[slot, u // 4, pl.ds(pl.multiple_of((u % 4) * 32, 32), 32)]

    def scatter(k, c):
        return remote(unit_of(OWN, c), relay.at[k], scat_s.at[k, c], scat_r.at[k], at_place(plane + 4 + c))

    here = (2 + zhi, 3 - zhi)
    there = (2 + ((z + 1) % NZ) // 16, 3 - ((z + NZ - 1) % NZ) // 16)

    def relayed(k, u, slot):
        return remote(relay.at[k], unit_of(slot, u), wrap_s.at[k], wrap_r.at[k, u], at_place(beyond[k]))

    def wait_units(k, rows_from):
        def one(v, _):
            relayed(k, (v // 2) * 4 + rows_from + v % 2, here[k]).wait_recv()
            return _

        lax.fori_loop(0, 4, one, 0)

    def on_side(wrapped, fn):
        for k in range(2):
            @pl.when(wrapped & (at_lo if k == 0 else at_hi))
            def _():
                fn(k)

    for j in range(CHUNKS // 2):
        for d in range(2):
            hop(0, d, j, first=True).start()
    for k in range(2):
        @pl.when(xy == ends[k])
        def _():
            def one(c, _):
                scatter(k, c).start()
                return _

            lax.fori_loop(0, 8, one, 0)

    @pl.when(jnp.logical_not(wrap_prev))
    def _():
        for j in range(CHUNKS // 2, CHUNKS):
            for d in range(2):
                to_before(d, j).start()

    @pl.when(jnp.logical_not(wrap_next))
    def _():
        for d in range(2):
            to_after(d).start()

    @pl.when(jnp.logical_not(wrap_prev))
    def _():
        for j in range(CHUNKS // 2):
            for d in range(2):
                to_before(d, j).start()

    own_to_sib.start()

    def flow(d, src=None):
        return remote(
            xbuf.at[d] if src is None else src, xbuf.at[d], flow_s.at[d], flow_r.at[d], up if d == 0 else down
        )

    for k in range(2):
        @pl.when(mover == 1)
        def _():
            scatter(k, xy - 4).wait_recv()
            relayed(k, xy - 4, there[k]).start()

            @pl.when((carrier == 1) & (gone[1 - k] == 0))
            def _():
                flow(1 - k, relay.at[k]).start()

    def forward(h, parts=(0, 2, 1, 3), last=False):
        for j in parts:
            for d in range(2):
                hop(h - 1, d, j, first=True).wait_recv()
                hop(h, d, j, last=last).start()

    def forward_xtra(h):
        for d in range(2):
            @pl.when((carrier == 1) & (gone[d] == h))
            def _():
                flow(d).wait_recv()
                flow(d).start()

    def xtra_rows(d, v):
        return pl.ds(pl.multiple_of((d + zhi - 2 * d * zhi) * half + (v % 2) * 32, 32), 32)

    def drop(d, v):
        return remote(
            xbuf.at[d], early.at[XTRA, v // 2, xtra_rows(d, v)], drop_s.at[d], xtra_r.at[d, v], at_place(z + 240)
        )

    mine = (xy // 4 - 1) * 2 + xy % 2

    FRONT, BACK = (0, 1), (2, 3)
    forward(1, FRONT)

    @pl.when(jnp.logical_not(wrap_next))
    def _():
        for j in BACK:
            for d in range(2):
                to_before(d, j).wait_recv()

    on_side(wrap_next, lambda k: wait_units(k, 2))
    for j in BACK:
        for d in range(2):
            hop(0, d, j, first=True).start()

    def unit(i, y, diagonal=None):
        s = lax.dot_general(
            early[OWN, i], y, (((1,), (1,)), ((), ())), preferred_element_type=F32
        )
        u = scale * s + offset
        if diagonal is not None:
            same = lax.broadcasted_iota(jnp.int32, u.shape, 0) == lax.broadcasted_iota(jnp.int32, u.shape, 1)
            flip = jnp.where(same, 1.0 - 2.0 * diagonal, 1.0)
            u = u * flip
        e = jnp.exp(-jnp.abs(u))
        c = scale * (jnp.where(u >= 0, 1.0, e) / (1.0 + e))
        if diagonal is not None:
            c = c * flip
        acc[i] += jnp.dot(c.astype(BF16), y, preferred_element_type=F32)
        if i == 0:
            loss_acc[...] += jnp.maximum(u, 0.0) + jnp.log1p(e)

    def skewed(h, _):
        forward(h, FRONT)
        forward(h - 1, BACK)
        forward_xtra(h - 1)
        return _

    lax.fori_loop(2, 6, skewed, 0)
    forward(5, BACK)
    forward_xtra(5)

    own_to_sib.wait_recv()

    @pl.when(jnp.logical_not(wrap_next))
    def _():
        for d in range(2):
            for j in FRONT:
                to_before(d, j).wait_recv()

    @pl.when(jnp.logical_not(wrap_prev))
    def _():
        for d in range(2):
            to_after(d).wait_recv()

    on_side(wrap_next, lambda k: wait_units(k, 0))

    def all_units(k):
        wait_units(k, 0)
        wait_units(k, 2)

    on_side(wrap_prev, all_units)

    @pl.when(inner * (1 - role) == 0)
    def _():
        edge_to_sib.start()

    def with_unit(p, carry):
        diagonal = jnp.where(p == 0, 1.0, 0.0).astype(F32)
        used = inner * (p // 3) == 0
        for i in range(2):
            forward(6 + 2 * p + i)
            forward_xtra(6 + 2 * p + i)

            @pl.when(used)
            def _():
                unit(i, early[p, 1 - i], diagonal)
        return carry

    lax.fori_loop(0, 4, with_unit, 0)
    edge_early = inner * role == 0

    @pl.when(edge_early)
    def _():
        edge_to_sib.wait_recv()

    for i in range(2):
        forward(14 + i, last=i == 1)
        forward_xtra(14 + i)

        @pl.when(edge_early)
        def _():
            unit(i, early[EDGE, 1 - i])

    def part_rows(j):
        return pl.ds(pl.multiple_of(j * CH, CH), CH)

    def fwd_y(d, j):
        if j < CHUNKS // 2:
            src, dst, dev = j, j + 2 * inner, after
        else:
            src, dst, dev = j - 2 * outer, j - 2 * outer, before
        return remote(
            late_r.at[d, part_rows(src)], late_y.at[d, part_rows(dst)], fy_s.at[d, j], fy_r.at[d, dst], dev
        )

    def got_y(d, j):
        return remote(late_r.at[d, rows(j)], late_y.at[d, rows(j)], fy_s.at[d, j], fy_r.at[d, j], after)

    def fwd_rs(d, j, other=None):
        src = late_r.at[d, rows(j)] if other is None else early.at[other, d, rows(j)]
        return remote(src, late_r.at[d, rows(CHUNKS + j)], rs_s.at[d, j], rs_r.at[d, j], sibling)

    def fwd_ys(d, j, other=None):
        src = late_y.at[d, rows(j)] if other is None else early.at[other, d, rows(j)]
        return remote(src, late_y.at[d, rows(CHUNKS + j)], ys_s.at[d, j], ys_r.at[d, j], sibling)

    def either(copy, other, which):
        @pl.when(which)
        def _():
            copy(other).start()

        @pl.when(jnp.logical_not(which))
        def _():
            copy(None).start()

    outer_first, inner_second = outer * (1 - role) == 1, inner * role == 1
    chunks = [(d, j) for j in (0, 2, 1, 3) for d in range(2)]
    for d, j in chunks:
        hop(15, d, j, first=True, last=True).wait_recv()
        fwd_y(d, j).start()
        if j < CHUNKS // 2:
            fwd_rs(d, j).start()
        else:
            either(lambda other: fwd_rs(d, j, other), PREV, outer_first)

    for d in range(2):
        @pl.when(carrier * mid == 1)
        def _():
            @pl.when(gone[d] == 16)
            def _():
                flow(d).wait_recv()

        @pl.when(dropping)
        def _():
            drop(d, mine).start()

    @pl.when(inner == 1)
    def _():
        for d in range(2):
            def one(v, _):
                drop(d, v).wait_recv()
                return _

            lax.fori_loop(0, 4, one, 0)

        @pl.when(role == 0)
        def _():
            xtra_to_sib.start()

        for i in range(2):
            unit(i, early[XTRA, 1 - i])

    lo, hi = pl.ds(0, ROWS), pl.ds(ROWS, ROWS)
    for i in range(2):
        unit(i, late_r[1 - i, lo])
    for d, j in chunks:
        got_y(d, j).wait_recv()
        if j < CHUNKS // 2:
            either(lambda other: fwd_ys(d, j, other), PREV, outer_first)
        else:
            either(lambda other: fwd_ys(d, j, other), XTRA, inner_second)
    for d, j in chunks:
        fwd_rs(d, j).wait_recv()
    for i in range(2):
        unit(i, late_r[1 - i, hi])
        unit(i, late_y[1 - i, lo])

    @pl.when(inner * role == 1)
    def _():
        xtra_to_sib.wait_recv()
        for i in range(2):
            unit(i, early[EDGE, 1 - i])

    for d, j in chunks:
        fwd_ys(d, j).wait_recv()
    for i in range(2):
        unit(i, late_y[1 - i, hi])

    for dst, i in ((gimg_ref, 0), (gtxt_ref, 1)):
        for c in range(CHUNKS):
            r = pl.ds(c * CH, CH)
            x = emb[i, r, :]
            g = acc[i, r, :]
            inv = lax.rsqrt(jnp.sum(x * x, axis=1, keepdims=True) + 1e-06)
            x = x * inv
            dst[r, :] = (g - x * jnp.sum(x * g, axis=1, keepdims=True)) * inv
    loss_ref[...] = jnp.sum(loss_acc[...].T, axis=0) / (BLOCKS * ROWS)

    def sent(h, _):
        for d in range(2):
            for j in range(CHUNKS):
                hop(h, d, j, first=True).wait_send()
        return _

    lax.fori_loop(0, 15, sent, 0)
    for d, j in chunks:
        hop(15, d, j, first=True, last=True).wait_send()
        fwd_y(d, j).wait_send()
        fwd_rs(d, j).wait_send()
        fwd_ys(d, j).wait_send()

    @pl.when(jnp.logical_not(wrap_prev))
    def _():
        for d, j in chunks:
            to_before(d, j).wait_send()

    @pl.when(jnp.logical_not(wrap_next))
    def _():
        for d in range(2):
            to_after(d).wait_send()

    for k in range(2):
        @pl.when(xy == ends[k])
        def _():
            def one(c, _):
                scatter(k, c).wait_send()
                return _

            lax.fori_loop(0, 8, one, 0)

        @pl.when(mover == 1)
        def _():
            relayed(k, xy - 4, there[k]).wait_send()

    for d in range(2):
        @pl.when((carrier == 1) & (gone[d] <= 15))
        def _():
            flow(d).wait_send()

        @pl.when(dropping)
        def _():
            drop(d, mine).wait_send()

    own_to_sib.wait_send()
    edge_to_sib.wait_send()


def on_device(image_emb, text_emb, log_scale, bias):
    vmem, smem = pl.BlockSpec(memory_space=pltpu.VMEM), pl.BlockSpec(memory_space=pltpu.SMEM)
    dma = pltpu.SemaphoreType.DMA
    return pl.pallas_call(
        kernel,
        out_shape=(
            jax.ShapeDtypeStruct((ROWS,), F32),
            jax.ShapeDtypeStruct((ROWS, WIDTH), F32),
            jax.ShapeDtypeStruct((ROWS, WIDTH), F32),
        ),
        in_specs=[pl.BlockSpec(memory_space=pl.ANY)] * 2 + [smem, smem],
        out_specs=(vmem, vmem, vmem),
        scratch_shapes=[
            pltpu.VMEM((2, ROWS, WIDTH), F32),
            pltpu.VMEM((6, 2, ROWS, WIDTH), BF16),
            pltpu.VMEM((15, 2, ROWS, WIDTH), BF16),
            pltpu.VMEM((2, 2 * ROWS, WIDTH), BF16),
            pltpu.VMEM((2, 2 * ROWS, WIDTH), BF16),
            pltpu.VMEM((2, ROWS, WIDTH), F32),
            pltpu.VMEM((ROWS, ROWS), F32),
            pltpu.VMEM((2, 32, WIDTH), BF16),
            pltpu.VMEM((2, 32, WIDTH), BF16),
            dma((2, 2)),
            dma((16, 2, CHUNKS)), dma((16, 2, CHUNKS)),
            dma((2, CHUNKS)), dma((2, CHUNKS)),
            dma((2,)), dma((2,)),
            dma((2,)), dma((2,)),
            dma((2, CHUNKS)), dma((2, CHUNKS)),
            dma((2, CHUNKS)), dma((2, CHUNKS)),
            dma((2, CHUNKS)), dma((2, CHUNKS)),
            dma((2, 8)), dma((2,)), dma((2,)), dma((2, 8)),
            dma((2,)), dma((2,)), dma((2,)), dma((2, 4)),
        ],
        compiler_params=pltpu.CompilerParams(
            collective_id=0, has_side_effects=True, vmem_limit_bytes=55050240
        ),
    )(image_emb, text_emb, log_scale, bias)


def solution(mesh):
    in_specs = (P(("blk", "grp"), None), P(("blk", "grp"), None), P(), P())
    out_specs = (P(("blk", "grp")), P(("blk", "grp"), None), P(("blk", "grp"), None))
    return jax.shard_map(
        on_device, mesh=mesh, in_specs=in_specs, out_specs=out_specs, check_vma=False
    )
```

```python
import jax
import jax.numpy as jnp
from jax import lax
from jax.experimental import pallas as pl
from jax.experimental.pallas import tpu as pltpu
from jax.sharding import PartitionSpec as P

MESH = pl.DeviceIdType.MESH
F32 = jnp.float32
BF16 = jnp.bfloat16

ROWS = 128
WIDTH = 1152
BLOCKS = 9
NZ = 32
CHUNKS = 4
CH = ROWS // CHUNKS

OWN, SIB, PREV, NEXT, EDGE, XTRA = range(6)


def kernel(
    img_ref, txt_ref, ls_ref, bias_ref,
    loss_ref, gimg_ref, gtxt_ref,
    emb, early, ring, late_r, late_y, acc, loss_acc, relay, xbuf,
    in_sem, ring_s, ring_r, next_s, next_r, prev_s, prev_r, sib_s, sib_r,
    fy_s, fy_r, rs_s, rs_r, ys_s, ys_r,
    scat_s, scat_r, wrap_s, wrap_r, own_s, flow_s, flow_r, drop_s, xtra_r,
):
    blk, grp = lax.axis_index("blk"), lax.axis_index("grp")
    zhi, core = grp // 2, grp % 2
    zlo, xy = blk // 16, blk % 16
    z = zhi * 16 + zlo

    def at_z(zz):
        return {"blk": (zz % 16) * 16 + xy, "grp": (zz // 16) * 2 + core}

    up, down = at_z((z + 1) % NZ), at_z((z + NZ - 1) % NZ)
    side = 1 - 2 * zhi
    place = z * 16 + xy

    def at_place(p):
        return {"blk": p % 256, "grp": (p // 256) * 2 + core}

    after, before = at_place((place + side + 512) % 512), at_place((place - side + 512) % 512)
    sibling = {"blk": blk, "grp": grp + 1 - 2 * core}
    role = core + zhi - 2 * core * zhi
    inner = ((place + 1) // 256) * (1 - place // 257)
    outer = (511 - place) // 511 + place // 511
    carrier = (xy % 8) // 4
    mid = ((z + 1) // 16) * (1 - z // 17)
    itself = inner * (1 - zhi)
    dropping = carrier * mid * (1 - itself) == 1
    gone = (z, NZ - 1 - z)
    ahead = 1 - (xy % 12 + 11) // 12

    at_lo, at_hi = xy == 0, xy == 15
    wrap_next = xy == 15 * (1 - zhi)
    wrap_prev = xy == 15 * zhi
    ends = (15, 0)
    plane = z * 16
    beyond = ((plane + 16) % 512, (plane + 511) % 512)
    planes = ((plane + 496) % 512, (plane + 16) % 512)

    half = ROWS // 2
    loads = []
    for h in range(2):
        for src, i in ((img_ref, 0), (txt_ref, 1)):
            r = pl.ds(h * half, half)
            copy = pltpu.make_async_copy(src.at[r], emb.at[i, r], in_sem.at[i, h])
            copy.start()
            loads.append((copy, i, h))

    barrier = pltpu.get_barrier_semaphore()

    def greet(dev):
        pl.semaphore_signal(barrier, inc=1, device_id=dev, device_id_type=MESH)

    for dev in (up, down, after, before, sibling):
        greet(dev)
    count = 7 + 14 * (xy // 15) + 14 * ((15 - xy) // 15) + carrier * mid * (1 - itself)
    for k in range(2):
        is_end = xy == ends[k]

        @pl.when(jnp.logical_not(is_end))
        def _():
            greet(at_place(plane + ends[k]))

        @pl.when(xy == ends[1 - k])
        def _():
            def one(c, _):
                greet(at_place(planes[k] + c + k))
                return _

            lax.fori_loop(0, 15, one, 0)

    @pl.when(inner == 1)
    def _():
        def one(v, _):
            greet(at_place(plane + (v // 4) * 8 + 4 + v % 4))
            return _

        lax.fori_loop(0, 7 + zhi, one, 0)

    for copy, i, h in loads:
        copy.wait()
        for c in range(2):
            r = pl.ds(h * half + c * CH, CH)
            x = emb[i, r, :]
            inv = lax.rsqrt(jnp.sum(x * x, axis=1, keepdims=True) + 1e-06)
            early[OWN, i, r, :] = (x * inv).astype(BF16)
    scale = jnp.exp(jnp.full((1, 128), ls_ref[0], F32))
    offset = bias_ref[0]

    pl.semaphore_wait(barrier, count)

    def remote(src, dst, ss, rs, dev):
        return pltpu.make_async_remote_copy(
            src_ref=src, dst_ref=dst, send_sem=ss, recv_sem=rs, device_id=dev, device_id_type=MESH
        )

    def rows(j):
        return pl.ds(j * CH, CH)

    def hop(h, d, j, first=False, last=False):
        if first:
            src = early.at[OWN if j < CHUNKS // 2 else NEXT, d, rows(j)]
        else:
            src = ring.at[h - 1, d, rows(j)]
        dst = late_r.at[d, rows(j)] if last else ring.at[h, d, rows(j)]
        return remote(src, dst, ring_s.at[h, d, j], ring_r.at[h, d, j], up if d == 0 else down)

    def to_before(d, j):
        return remote(
            early.at[OWN, d, rows(j)], early.at[NEXT, d, rows(j)], next_s.at[d, j], next_r.at[d, j], before
        )

    def to_after(d):
        return remote(early.at[OWN, d], early.at[PREV, d], prev_s.at[d], prev_r.at[d], after)

    own_to_sib = remote(early.at[OWN], early.at[SIB], sib_s.at[0], sib_r.at[0], sibling)
    edge_to_sib = remote(early.at[NEXT - role], early.at[EDGE], sib_s.at[1], sib_r.at[1], sibling)
    xtra_to_sib = remote(early.at[XTRA], early.at[EDGE], sib_s.at[1], sib_r.at[1], sibling)

    def unit_of(slot, u):
        return early.at[slot, u // 8, pl.ds(pl.multiple_of((u % 8) * 16, 16), 16)]

    def scatter(k, c):
        return remote(unit_of(OWN, c), relay.at[k], scat_s.at[k, c], scat_r.at[k], at_place(plane + c))

    here = (2 + zhi, 3 - zhi)
    there = (2 + ((z + 1) % NZ) // 16, 3 - ((z + NZ - 1) % NZ) // 16)

    def relayed(k, u, slot):
        return remote(relay.at[k], unit_of(slot, u), wrap_s.at[k], wrap_r.at[k, u], at_place(beyond[k]))

    def straight(k):
        return remote(
            unit_of(OWN, ends[k]), unit_of(there[k], ends[k]), own_s.at[k], wrap_r.at[k, ends[k]], at_place(beyond[k])
        )

    def wait_units(k, rows_from):
        def one(v, _):
            relayed(k, (v // 4) * 8 + rows_from + v % 4, here[k]).wait_recv()
            return _

        lax.fori_loop(0, 8, one, 0)

    def on_side(wrapped, fn):
        for k in range(2):
            @pl.when(wrapped & (at_lo if k == 0 else at_hi))
            def _():
                fn(k)

    for j in range(CHUNKS // 2):
        for d in range(2):
            hop(0, d, j, first=True).start()
    for k in range(2):
        @pl.when(xy == ends[k])
        def _():
            straight(k).start()

            def one(c, _):
                scatter(k, c + k).start()
                return _

            lax.fori_loop(0, 15, one, 0)

    @pl.when(jnp.logical_not(wrap_prev))
    def _():
        for j in range(CHUNKS // 2, CHUNKS):
            for d in range(2):
                to_before(d, j).start()

    @pl.when(jnp.logical_not(wrap_next))
    def _():
        for d in range(2):
            to_after(d).start()

    @pl.when(jnp.logical_not(wrap_prev))
    def _():
        for j in range(CHUNKS // 2):
            for d in range(2):
                to_before(d, j).start()

    own_to_sib.start()

    def flow(d, src=None):
        return remote(
            xbuf.at[d] if src is None else src, xbuf.at[d], flow_s.at[d], flow_r.at[d], up if d == 0 else down
        )

    for k in range(2):
        @pl.when(xy != ends[k])
        def _():
            scatter(k, xy).wait_recv()
            relayed(k, xy, there[k]).start()

            @pl.when((carrier == 1) & (gone[1 - k] == 0))
            def _():
                flow(1 - k, relay.at[k]).start()

    @pl.when(place == 511)
    def _():
        flow(1, unit_of(OWN, 15)).start()

    def forward(h, parts=(0, 2, 1, 3), last=False):
        for j in parts:
            for d in range(2):
                hop(h - 1, d, j, first=True).wait_recv()
                hop(h, d, j, last=last).start()

    def forward_xtra(h):
        for d in range(2):
            @pl.when((carrier == 1) & (gone[d] == h))
            def _():
                flow(d).wait_recv()
                flow(d).start()

    def xtra_rows(d, v):
        return pl.ds(pl.multiple_of((d + zhi - 2 * d * zhi) * half + (v % 4) * 16, 16), 16)

    def drop(d, v):
        return remote(
            xbuf.at[d], early.at[XTRA, v // 4, xtra_rows(d, v)], drop_s.at[d], xtra_r.at[d, v], at_place(z + 240)
        )

    mine = (xy // 8) * 4 + xy % 4

    FRONT, BACK = (0, 1), (2, 3)
    forward(1, FRONT)

    @pl.when(ahead == 1)
    def _():
        forward(2, FRONT)

    @pl.when(jnp.logical_not(wrap_next))
    def _():
        for j in BACK:
            for d in range(2):
                to_before(d, j).wait_recv()

    on_side(wrap_next, lambda k: wait_units(k, 4))
    for j in BACK:
        for d in range(2):
            hop(0, d, j, first=True).start()

    def unit(i, y, diagonal=None):
        s = lax.dot_general(
            early[OWN, i], y, (((1,), (1,)), ((), ())), preferred_element_type=F32
        )
        u = scale * s + offset
        if diagonal is not None:
            same = lax.broadcasted_iota(jnp.int32, u.shape, 0) == lax.broadcasted_iota(jnp.int32, u.shape, 1)
            flip = jnp.where(same, 1.0 - 2.0 * diagonal, 1.0)
            u = u * flip
        e = jnp.exp(-jnp.abs(u))
        c = scale * (jnp.where(u >= 0, 1.0, e) / (1.0 + e))
        if diagonal is not None:
            c = c * flip
        acc[i] += jnp.dot(c.astype(BF16), y, preferred_element_type=F32)
        if i == 0:
            loss_acc[...] += jnp.maximum(u, 0.0) + jnp.log1p(e)

    def skewed(h, _):
        forward(h + ahead, FRONT)
        forward(h - 1, BACK)
        forward_xtra(h - 1)
        return _

    acc[...] = jnp.zeros_like(acc)
    loss_acc[...] = jnp.zeros_like(loss_acc)
    lax.fori_loop(2, 6, skewed, 0)
    forward(5, BACK)
    forward_xtra(5)

    own_to_sib.wait_recv()

    @pl.when(jnp.logical_not(wrap_next))
    def _():
        for d in range(2):
            for j in FRONT:
                to_before(d, j).wait_recv()

    @pl.when(jnp.logical_not(wrap_prev))
    def _():
        for d in range(2):
            to_after(d).wait_recv()

    on_side(wrap_next, lambda k: wait_units(k, 0))

    def all_units(k):
        wait_units(k, 0)
        wait_units(k, 4)

    on_side(wrap_prev, all_units)

    @pl.when(inner * (1 - role) == 0)
    def _():
        edge_to_sib.start()

    def with_unit(p, carry):
        diagonal = jnp.where(p == 0, 1.0, 0.0).astype(F32)
        used = inner * (p // 3) == 0
        for i in range(2):
            if i == 0:
                @pl.when((p == 0) & (ahead == 1))
                def _():
                    forward(6, BACK)

                @pl.when((p > 0) | (ahead == 0))
                def _():
                    forward(6 + 2 * p)
            else:
                forward(7 + 2 * p)
            forward_xtra(6 + 2 * p + i)

            @pl.when(used)
            def _():
                unit(i, early[p, 1 - i], diagonal)
        return carry

    lax.fori_loop(0, 4, with_unit, 0)
    edge_early = inner * role == 0

    @pl.when(edge_early)
    def _():
        edge_to_sib.wait_recv()

    for i in range(2):
        forward(14 + i, last=i == 1)
        forward_xtra(14 + i)

        @pl.when(edge_early)
        def _():
            unit(i, early[EDGE, 1 - i])

    def part_rows(j):
        return pl.ds(pl.multiple_of(j * CH, CH), CH)

    def fwd_y(d, j):
        if j < CHUNKS // 2:
            src, dst, dev = j, j + 2 * inner, after
        else:
            src, dst, dev = j - 2 * outer, j - 2 * outer, before
        return remote(
            late_r.at[d, part_rows(src)], late_y.at[d, part_rows(dst)], fy_s.at[d, j], fy_r.at[d, dst], dev
        )

    def got_y(d, j):
        return remote(late_r.at[d, rows(j)], late_y.at[d, rows(j)], fy_s.at[d, j], fy_r.at[d, j], after)

    def fwd_rs(d, j, other=None):
        src = late_r.at[d, rows(j)] if other is None else early.at[other, d, rows(j)]
        return remote(src, late_r.at[d, rows(CHUNKS + j)], rs_s.at[d, j], rs_r.at[d, j], sibling)

    def fwd_ys(d, j, other=None):
        src = late_y.at[d, rows(j)] if other is None else early.at[other, d, rows(j)]
        return remote(src, late_y.at[d, rows(CHUNKS + j)], ys_s.at[d, j], ys_r.at[d, j], sibling)

    def either(copy, other, which):
        @pl.when(which)
        def _():
            copy(other).start()

        @pl.when(jnp.logical_not(which))
        def _():
            copy(None).start()

    outer_first, inner_second = outer * (1 - role) == 1, inner * role == 1
    chunks = [(d, j) for j in (0, 2, 1, 3) for d in range(2)]
    for d, j in chunks:
        hop(15, d, j, first=True, last=True).wait_recv()
        fwd_y(d, j).start()
        if j < CHUNKS // 2:
            fwd_rs(d, j).start()
        else:
            either(lambda other: fwd_rs(d, j, other), PREV, outer_first)

    for d in range(2):
        @pl.when(carrier * mid == 1)
        def _():
            @pl.when(gone[d] == 16)
            def _():
                flow(d).wait_recv()

        @pl.when(dropping)
        def _():
            drop(d, mine).start()

        @pl.when(itself == 1)
        def _():
            early[XTRA, 1, pl.ds(d * half + 48, 16), :] = xbuf[d]

    @pl.when(inner == 1)
    def _():
        for d in range(2):
            def one(v, _):
                drop(d, v).wait_recv()
                return _

            lax.fori_loop(0, 7 + zhi, one, 0)

        @pl.when(role == 0)
        def _():
            xtra_to_sib.start()

        for i in range(2):
            unit(i, early[XTRA, 1 - i])

    lo, hi = pl.ds(0, ROWS), pl.ds(ROWS, ROWS)
    for i in range(2):
        unit(i, late_r[1 - i, lo])
    for d, j in chunks:
        got_y(d, j).wait_recv()
        if j < CHUNKS // 2:
            either(lambda other: fwd_ys(d, j, other), PREV, outer_first)
        else:
            either(lambda other: fwd_ys(d, j, other), XTRA, inner_second)
    for d, j in chunks:
        fwd_rs(d, j).wait_recv()
    for i in range(2):
        unit(i, late_r[1 - i, hi])
        unit(i, late_y[1 - i, lo])

    @pl.when(inner * role == 1)
    def _():
        xtra_to_sib.wait_recv()
        for i in range(2):
            unit(i, early[EDGE, 1 - i])

    for d, j in chunks:
        fwd_ys(d, j).wait_recv()
    for i in range(2):
        unit(i, late_y[1 - i, hi])

    for dst, i in ((gimg_ref, 0), (gtxt_ref, 1)):
        for c in range(CHUNKS):
            r = pl.ds(c * CH, CH)
            x = emb[i, r, :]
            g = acc[i, r, :]
            inv = lax.rsqrt(jnp.sum(x * x, axis=1, keepdims=True) + 1e-06)
            x = x * inv
            dst[r, :] = (g - x * jnp.sum(x * g, axis=1, keepdims=True)) * inv
    loss_ref[...] = jnp.sum(loss_acc[...].T, axis=0) / (BLOCKS * ROWS)

    def sent(h, _):
        for d in range(2):
            for j in range(CHUNKS):
                hop(h, d, j, first=True).wait_send()
        return _

    lax.fori_loop(0, 15, sent, 0)
    for d, j in chunks:
        hop(15, d, j, first=True, last=True).wait_send()
        fwd_y(d, j).wait_send()
        fwd_rs(d, j).wait_send()
        fwd_ys(d, j).wait_send()

    @pl.when(jnp.logical_not(wrap_prev))
    def _():
        for d, j in chunks:
            to_before(d, j).wait_send()

    @pl.when(jnp.logical_not(wrap_next))
    def _():
        for d in range(2):
            to_after(d).wait_send()

    for k in range(2):
        @pl.when(xy == ends[k])
        def _():
            straight(k).wait_send()

            def one(c, _):
                scatter(k, c + k).wait_send()
                return _

            lax.fori_loop(0, 15, one, 0)

        @pl.when(xy != ends[k])
        def _():
            relayed(k, xy, there[k]).wait_send()

    for d in range(2):
        @pl.when((carrier == 1) & (gone[d] <= 15))
        def _():
            flow(d).wait_send()

        @pl.when(dropping)
        def _():
            drop(d, mine).wait_send()

    own_to_sib.wait_send()
    edge_to_sib.wait_send()


def on_device(image_emb, text_emb, log_scale, bias):
    vmem, smem = pl.BlockSpec(memory_space=pltpu.VMEM), pl.BlockSpec(memory_space=pltpu.SMEM)
    dma = pltpu.SemaphoreType.DMA
    return pl.pallas_call(
        kernel,
        out_shape=(
            jax.ShapeDtypeStruct((ROWS,), F32),
            jax.ShapeDtypeStruct((ROWS, WIDTH), F32),
            jax.ShapeDtypeStruct((ROWS, WIDTH), F32),
        ),
        in_specs=[pl.BlockSpec(memory_space=pl.ANY)] * 2 + [smem, smem],
        out_specs=(vmem, vmem, vmem),
        scratch_shapes=[
            pltpu.VMEM((2, ROWS, WIDTH), F32),
            pltpu.VMEM((6, 2, ROWS, WIDTH), BF16),
            pltpu.VMEM((15, 2, ROWS, WIDTH), BF16),
            pltpu.VMEM((2, 2 * ROWS, WIDTH), BF16),
            pltpu.VMEM((2, 2 * ROWS, WIDTH), BF16),
            pltpu.VMEM((2, ROWS, WIDTH), F32),
            pltpu.VMEM((ROWS, ROWS), F32),
            pltpu.VMEM((2, 16, WIDTH), BF16),
            pltpu.VMEM((2, 16, WIDTH), BF16),
            dma((2, 2)),
            dma((16, 2, CHUNKS)), dma((16, 2, CHUNKS)),
            dma((2, CHUNKS)), dma((2, CHUNKS)),
            dma((2,)), dma((2,)),
            dma((2,)), dma((2,)),
            dma((2, CHUNKS)), dma((2, CHUNKS)),
            dma((2, CHUNKS)), dma((2, CHUNKS)),
            dma((2, CHUNKS)), dma((2, CHUNKS)),
            dma((2, 16)), dma((2,)), dma((2,)), dma((2, 16)), dma((2,)),
            dma((2,)), dma((2,)), dma((2,)), dma((2, 8)),
        ],
        compiler_params=pltpu.CompilerParams(
            collective_id=0, has_side_effects=True, vmem_limit_bytes=55050240
        ),
    )(image_emb, text_emb, log_scale, bias)


def solution(mesh):
    in_specs = (P(("blk", "grp"), None), P(("blk", "grp"), None), P(), P())
    out_specs = (P(("blk", "grp")), P(("blk", "grp"), None), P(("blk", "grp"), None))
    return jax.shard_map(
        on_device, mesh=mesh, in_specs=in_specs, out_specs=out_specs, check_vma=False
    )
```
